128 devices in a mesh: layer: 2 (over core), row: 4 (over y), col: 16 (over z, x).
Axes of the slice: x: 4, y: 4, z: 4, core: 2. Of those that a mesh axis runs over, the one named last changes fastest.
Arguments:
- values: bfloat16 [2048, 24, 128, 128], P(('row', 'col'), 'layer'), may hold values from -0.15625 to 0.15625
- cols: int32 [2048, 24], P(('row', 'col'), 'layer'), may hold values from 0 to 2047, as said below
- counts: int32 [2048], P(('row', 'col')), may hold values from 1 to 24, as said below
- vectors: bfloat16 [262144, 512], P(('row', 'col')), may hold values from -6 to 6
Outputs:
- result: float32 [262144, 512], P(('row', 'col'), 'layer')
The draws below stay inside these ranges and needn't reach their ends.
Inputs may be any that keep to these rules, and one draw needn't show every extreme that they name: cols[i, k] lies within 16 of i; on every device whose rows have such neighbours, some block row has its slot 0 exactly 16 below the diagonal and some exactly 16 above. `counts`: slot 0 is always present; every device has a block row with all 24 slots present.
All inputs are finite; a program needn't handle non-finite values.
Results may differ from the reference program's by a relative error of at most 0.0018.
Values may be sent and summed in bfloat16 or wider, within the bound.
No kernel may reach another device: no remote copies, remote signals or barrier semaphores. Data moves between devices by JAX's collectives and lax.ppermute only.
A program may use at most 192 MiB of HBM per device.

```python
import jax
import jax.numpy as jnp
from jax import lax

BS = 128
RB = 32
KB = 24
BAND = 16
NB = 2048
S = 512


def draw_cols(key, part):
    key = jax.random.fold_in(key, 11)
    rows = jnp.arange(NB, dtype=jnp.int32)[:, None]
    lower = jnp.maximum(rows - BAND, 0)
    upper = jnp.minimum(rows + BAND, NB - 1)
    offsets = jax.random.randint(key, (NB, KB), 0, 2 * BAND + 1)
    picked = lower + offsets % (upper - lower + 1)
    slot_zero = jnp.arange(KB, dtype=jnp.int32)[None, :] == 0
    below = jnp.logical_and(rows % RB == 0, rows >= BAND)
    above = jnp.logical_and(rows % RB == RB - 1, rows + BAND < NB)
    picked = jnp.where(jnp.logical_and(slot_zero, below), rows - BAND, picked)
    picked = jnp.where(jnp.logical_and(slot_zero, above), rows + BAND, picked)
    return picked.astype(jnp.int32)


def draw_counts(key, part):
    key = jax.random.fold_in(key, 12)
    rows = jnp.arange(NB, dtype=jnp.int32)
    drawn = jax.random.randint(key, (NB,), 1, KB + 1)
    return jnp.where(rows % RB == 1, KB, drawn).astype(jnp.int32)


def block_scale(rng, shape, cuts, low, top_value):
    level, own = 1.0, jax.random.fold_in(rng, 6)
    for position, parts in cuts:
        steps = jnp.exp(jax.random.uniform(jax.random.fold_in(own, position), (parts,), jnp.float32, low / len(cuts), top_value / len(cuts)))
        level = level * jnp.repeat(steps, shape[position] // parts).reshape([-1 if axis == position else 1 for axis in range(len(shape))])
    return level


def scatter_about(own_key, extent, width, reach, cuts=(), kind=jnp.bfloat16):
    values = jax.random.normal(own_key, extent, jnp.float32) * width
    if len(cuts) > 0:
        values = block_scale(own_key, extent, cuts, -0.22, 0.18) * values
    return jnp.clip(values, min=-reach, max=reach).astype(kind)


def setup_inputs(seed: int = 0) -> dict:
    arg_keys = jax.random.split(jax.random.key(seed), 5)
    values = scatter_about(arg_keys[0], (NB, KB, BS, BS), (KB * BS // 2) ** -0.5, 0.15625, ((0, 64), (1, 2)))
    cols = draw_cols(jax.random.fold_in(arg_keys[4], 71), 0)
    counts = draw_counts(jax.random.fold_in(arg_keys[4], 71), 0)
    vectors = scatter_about(arg_keys[3], (NB * BS, S), 1.0, 6.0, ((0, 64),))
    return {"values": values, "cols": cols, "counts": counts, "vectors": vectors}


def apply_matrix(values, cols, present, field):
    stacked = field.reshape(NB, BS, S)
    masked = values * present[:, :, None, None]
    groups_vals = masked.reshape(NB // RB, RB, KB, BS, BS)
    groups_cols = cols.reshape(NB // RB, RB, KB)

    def one_group(pair):
        block_vals, block_cols = pair
        picked = stacked[block_cols].astype(jnp.float32)
        return jnp.einsum("rkab,rkbs->ras", block_vals.astype(jnp.float32), picked)

    out = lax.map(one_group, (groups_vals, groups_cols))
    return out.reshape(NB * BS, S)


def reference(values, cols, counts, vectors):
    slots = jnp.arange(KB, dtype=jnp.int32)[None, :]
    present = (slots < counts[:, None]).astype(jnp.bfloat16)
    first = apply_matrix(values, cols, present, vectors)
    second = apply_matrix(values, cols, present, first.astype(jnp.bfloat16))
    third = apply_matrix(values, cols, present, second.astype(jnp.bfloat16))
    return 1.5 * first - 0.5 * third
```

```python
import functools

import jax
import jax.numpy as jnp
from jax import lax
from jax.experimental import pallas as pl
from jax.experimental.pallas import tpu as pltpu
from jax.sharding import PartitionSpec as P

AXES = ("layer", "row", "col")
GROUP = 4
TOGETHER = 4
F32, BF16 = jnp.float32, jnp.bfloat16
ANY = pl.BlockSpec(memory_space=pl.ANY)
SCALARS = pl.BlockSpec(memory_space=pltpu.SMEM)
RESIDENT = pl.BlockSpec(memory_space=pltpu.VMEM)


def in_vmem(x):
    return pltpu.with_memory_space_constraint(x, pltpu.VMEM)


def in_hbm(x):
    return pltpu.with_memory_space_constraint(x, pltpu.HBM)


def run_copies(copies):
    for copy in copies:
        copy.start()
    for copy in copies:
        copy.wait()


def stage_columns(vec, meta, own, after=()):
    rows, size, columns = vec.shape[0] // 2, vec.shape[1], vec.shape[2] // 2
    half = columns // 2

    def kernel(meta, vec, *refs):
        left, right, whole, sems = refs[-4:]
        at = (meta[0] if own else 1 - meta[0]) * rows
        run_copies([pltpu.make_async_copy(vec.at[pl.ds(at, rows)], whole, sems.at[0, 0])])
        run_copies(
            [
                pltpu.make_async_copy(
                    whole.at[:, :, pl.ds((2 * h + piece) * half, half)], out.at[:, :, pl.ds(h * half, half)], sems.at[1 + piece, h]
                )
                for piece, out in enumerate((left, right))
                for h in range(2)
            ]
        )

    shape = (rows, size, columns)
    return pl.pallas_call(
        kernel,
        out_shape=[jax.ShapeDtypeStruct(shape, BF16) if own else pltpu.VMEM(shape, BF16)] * 2,
        in_specs=[SCALARS, ANY] + [ANY] * len(after),
        out_specs=[ANY if own else RESIDENT] * 2,
        scratch_shapes=[pltpu.VMEM((rows, size, 2 * columns), BF16), pltpu.SemaphoreType.DMA((3, 2))],
        compiler_params=pltpu.CompilerParams(vmem_limit_bytes=3 * 2**20),
        cost_estimate=pl.CostEstimate(flops=0, bytes_accessed=1024, transcendentals=0),
        name="stage_columns",
    )(meta, in_hbm(vec), *after)


def fill_own(values, meta, after):
    rows, slots, size = values.shape[0] // 2, values.shape[1], values.shape[2]

    def kernel(meta, values, after, blocks, sem):
        for side in range(2):

            @pl.when(meta[0] == side)
            def _():
                run_copies(
                    [
                        pltpu.make_async_copy(
                            values.at[pl.ds(side * rows, rows)], blocks.at[:, pl.ds(side * slots, slots)], sem.at[side]
                        )
                    ]
                )

    return pl.pallas_call(
        kernel,
        out_shape=pltpu.VMEM((rows, 2 * slots, size, size), BF16),
        in_specs=[SCALARS, ANY, ANY],
        out_specs=RESIDENT,
        scratch_shapes=[pltpu.SemaphoreType.DMA((2,))],
        compiler_params=pltpu.CompilerParams(vmem_limit_bytes=4 * 2**20),
        cost_estimate=pl.CostEstimate(flops=0, bytes_accessed=1024, transcendentals=0),
        name="fill_own",
    )(meta, in_hbm(values), after)


def product_kernel(step, chunk, filling, tab, cnt, order, meta, *refs):
    lay = meta[0]
    refs = list(refs)
    take = lambda n: [refs.pop(0) for _ in range(n)]
    (blocks,) = take(1)
    other = take(1)[0] if filling else None
    mine, partner, halo = take(3)
    if step == 2:
        first, earlier, target = take(3)
    if filling:
        (blocks,) = take(1)
    outs = take({0: 2, 1: 1, 2: 2}[step])
    field, in_sems = take(2)
    if step == 2:
        kept, first_buf, out_sems = take(3)
    rows, half = halo.shape[0], halo.shape[2] // 2
    slots = blocks.shape[1] // 2

    copies = [
        pltpu.make_async_copy(part, field.at[pl.ds(n * rows, rows)], in_sems.at[n])
        for n, part in enumerate((halo, mine, partner))
    ]
    if step == 2:
        copies.append(pltpu.make_async_copy(first, first_buf, in_sems.at[3]))
        if earlier is not None:
            copies.append(
                pltpu.make_async_copy(
                    earlier, outs[0].at[pl.ds((1 - lay) * rows, rows), :, pl.ds(0, half)], in_sems.at[4]
                )
            )
    if filling:
        for side in range(2):

            @pl.when(lay == side)
            def _():
                run_copies(
                    [
                        pltpu.make_async_copy(
                            other.at[pl.ds(side * rows, rows)],
                            blocks.at[:, pl.ds((1 - side) * slots, slots)],
                            in_sems.at[5 + side],
                        )
                    ]
                )

    run_copies(copies)

    def keeping(r):
        place = outs[0].at[lay * rows + r, :, pl.ds(chunk * half, half)]
        return pltpu.make_async_copy(kept.at[r], place, out_sems.at[r])

    def emit(r, total):
        if step < 2:
            outs[-1][r] = total.astype(BF16)
        if step == 0:
            outs[0][r] = total
        if step == 2:
            final = 1.5 * first_buf[r] - 0.5 * total
            left, right = final[:, :half], final[:, half:]
            kept[r] = jnp.where(lay == 0, left, right)
            outs[1][r] = jnp.where(lay == 0, right, left)

    def some_rows(i, carry):
        picked = [order[i * TOGETHER + j] for j in range(TOGETHER)]
        counts = [cnt[r] for r in picked]
        used = (counts[0] + (GROUP - 1)) // GROUP
        for m in range(1, 2 * slots // GROUP + 1):

            @pl.when(used == m)
            def _():
                for r, count in zip(picked, counts):
                    left, right = [], []
                    for k in range(m * GROUP):
                        block = blocks[r, k]
                        left.append(jnp.where(k < count, block, jnp.zeros_like(block)))
                        right.append(field[tab[r * 2 * slots + k]])
                    emit(
                        r,
                        jnp.dot(
                            jnp.concatenate(left, axis=1), jnp.concatenate(right, axis=0), preferred_element_type=F32
                        ),
                    )

        if step == 2:
            for r in picked:
                keeping(r).start()
        return carry

    lax.fori_loop(0, rows // TOGETHER, some_rows, 0)

    def finish(r, carry):
        keeping(r).wait()
        return carry

    if step == 2:
        lax.fori_loop(0, rows, finish, 0)


def product(step, chunk, tables, blocks, operands):
    halo = operands["halo"]
    rows, size, columns = halo.shape
    half = columns // 2
    filling = "other" in operands
    inputs = [in_vmem(blocks)]
    if filling:
        inputs.append(in_hbm(operands["other"]))
    inputs += [operands[n] for n in ("mine", "partner", "halo")]
    blank = step == 2 and operands["earlier"] is None
    struct = jax.ShapeDtypeStruct
    aliases, outs, out_specs = {}, [], []
    lead = len(tables)
    if filling:
        outs.append(pltpu.VMEM(blocks.shape, BF16))
        out_specs.append(RESIDENT)
        aliases[lead] = 0
    if step == 2:
        inputs.append(operands["first"])
        if not blank:
            inputs += [operands["earlier"], operands["target"]]
            aliases[lead + len(inputs) - 1] = 0
    shape = (rows, size, columns)
    narrow = (rows, size, half)
    extra = []
    if step == 2:
        results = [struct((2 * rows, size, columns), F32), pltpu.VMEM(narrow, F32)]
        result_specs = [ANY, RESIDENT]
        extra = [pltpu.VMEM(narrow, F32), pltpu.VMEM(shape, F32), pltpu.SemaphoreType.DMA((rows,))]
    else:
        results = [pltpu.VMEM(shape, F32)] * (step == 0) + [pltpu.VMEM(shape, BF16)]
        result_specs = [RESIDENT] * len(results)

    def kernel(*refs):
        refs = list(refs)
        if blank:
            refs[lead + len(inputs) : lead + len(inputs)] = [None, None]
        product_kernel(step, chunk, filling, *refs)

    return pl.pallas_call(
        kernel,
        out_shape=outs + results,
        in_specs=[SCALARS] * len(tables) + [RESIDENT] + [ANY] * (len(inputs) - 1),
        out_specs=out_specs + result_specs,
        scratch_shapes=[
            pltpu.VMEM((3 * rows, size, columns), BF16),
            pltpu.SemaphoreType.DMA((7,)),
        ]
        + extra,
        input_output_aliases=aliases,
        compiler_params=pltpu.CompilerParams(vmem_limit_bytes=(10 if step == 2 else 8) * 2**20),
        cost_estimate=pl.CostEstimate(flops=5 * 10**9, bytes_accessed=8 * 2**20, transcendentals=0),
        name=f"product_{step}",
    )(*tables, *inputs)


def body(chips, values, cols, counts, vectors):
    rows = values.shape[0] // 2
    slots, size = values.shape[1], values.shape[2]
    columns = vectors.shape[1] // 2
    half = columns // 2
    lay = lax.axis_index("layer")
    start = lax.axis_index(("row", "col")) * 2 * rows
    up = [(chips + i, i + 1) for i in range(chips - 1)]
    across = up + [(b, a) for a, b in up]
    within = [(i, chips + i) for i in range(chips)] + [(chips + i, i) for i in range(chips)]
    cross = lambda x: lax.ppermute(x, AXES, across)
    swap = lambda x: lax.ppermute(x, AXES, within)

    meta = lay.astype(jnp.int32).reshape(1)
    vec = vectors.reshape(2 * rows, size, 2 * columns)
    other = swap(values)
    halos = [None] * 2
    mine = list(stage_columns(vec, meta, True))
    for q in range(2):
        halos[q] = cross(mine[q])
    cols_other = swap(lax.dynamic_slice_in_dim(cols, (1 - lay) * rows, rows, axis=0))
    cols_own = lax.dynamic_slice_in_dim(cols, lay * rows, rows, axis=0)
    low = jnp.where(lay == 0, cols_own, cols_other)
    high = jnp.where(lay == 0, cols_other, cols_own)
    place = jnp.concatenate([low, high], axis=1) - start
    turned = jnp.where(place < rows, place + 2 * rows, jnp.where(place < 2 * rows, place, place - 2 * rows))
    tab = jnp.where(lay == 0, place + rows, turned).reshape(-1)
    cnt = lax.dynamic_slice_in_dim(counts, lay * rows, rows, axis=0)
    numbers = jnp.arange(rows, dtype=jnp.int32)
    key = cnt * rows + numbers
    rank = jnp.sum((key[None, :] > key[:, None]).astype(jnp.int32), axis=1)
    order = jnp.sum(jnp.where(rank[:, None] == numbers[None, :], numbers[:, None], 0), axis=0)
    tables = (tab, cnt, order, meta)
    partner = list(stage_columns(vec, meta, False, [tab]))
    blocks = fill_own(values, meta, tab)

    first = [None] * 2
    for q in range(2):
        operands = {"mine": mine[q], "partner": partner[q], "halo": halos[q]}
        if q == 0:
            blocks, first[q], mine[q] = product(0, q, tables, blocks, {**operands, "other": other})
        else:
            first[q], mine[q] = product(0, q, tables, blocks, operands)
        halos[q], partner[q] = cross(mine[q]), swap(mine[q])
    for q in range(2):
        (mine[q],) = product(1, q, tables, blocks, {"mine": mine[q], "partner": partner[q], "halo": halos[q]})
        halos[q], partner[q] = cross(mine[q]), swap(mine[q])
    target = None
    earlier = None
    for q in range(2):
        operands = {"mine": mine[q], "partner": partner[q], "halo": halos[q], "first": first[q]}
        target, send = product(2, q, tables, blocks, {**operands, "earlier": earlier, "target": target})
        earlier = swap(send)
    target = lax.dynamic_update_slice(target, earlier, ((1 - lay) * rows, 0, half))
    return target.reshape(2 * rows * size, columns)


def solution(mesh):
    chips = mesh.shape["row"] * mesh.shape["col"]
    return jax.shard_map(
        functools.partial(body, chips),
        mesh=mesh,
        in_specs=(
            P(("row", "col"), "layer", None, None),
            P(("row", "col"), "layer"),
            P(("row", "col")),
            P(("row", "col"), None),
        ),
        out_specs=P(("row", "col"), "layer"),
        check_vma=False,
    )
```

```python
import functools
import types

import jax
import jax.numpy as jnp
from jax import lax
from jax.experimental import pallas as pl
from jax.experimental.pallas import tpu as pltpu
from jax.sharding import PartitionSpec as P

AXES = ("layer", "row", "col")
GROUP = 4
TOGETHER = 4
F32, BF16 = jnp.float32, jnp.bfloat16
ANY = pl.BlockSpec(memory_space=pl.ANY)
SCALARS = pl.BlockSpec(memory_space=pltpu.SMEM)
RESIDENT = pl.BlockSpec(memory_space=pltpu.VMEM)


def in_vmem(x):
    return pltpu.with_memory_space_constraint(x, pltpu.VMEM)


def in_hbm(x):
    return pltpu.with_memory_space_constraint(x, pltpu.HBM)


def start_all(copies):
    for copy in copies:
        copy.start()


def wait_all(copies):
    for copy in copies:
        copy.wait()


def run_copies(copies):
    start_all(copies)
    wait_all(copies)


def small_cost():
    return pl.CostEstimate(flops=0, bytes_accessed=1024, transcendentals=0)


def stage_columns(vec, meta, own, after=()):
    rows, size, columns = vec.shape[0] // 2, vec.shape[1], vec.shape[2] // 2
    half = columns // 2

    def kernel(meta, vec, *refs):
        left, right, whole, sems = refs[-4:]
        at = (meta[0] if own else 1 - meta[0]) * rows
        run_copies([pltpu.make_async_copy(vec.at[pl.ds(at, rows)], whole, sems.at[0, 0])])
        run_copies(
            [
                pltpu.make_async_copy(
                    whole.at[:, :, pl.ds((2 * h + piece) * half, half)],
                    out.at[:, :, pl.ds(h * half, half)],
                    sems.at[1 + piece, h],
                )
                for piece, out in enumerate((left, right))
                for h in range(2)
            ]
        )

    shape = (rows, size, columns)
    return pl.pallas_call(
        kernel,
        out_shape=[jax.ShapeDtypeStruct(shape, BF16) if own else pltpu.VMEM(shape, BF16)] * 2,
        in_specs=[SCALARS, ANY] + [ANY] * len(after),
        out_specs=[ANY if own else RESIDENT] * 2,
        scratch_shapes=[pltpu.VMEM((rows, size, 2 * columns), BF16), pltpu.SemaphoreType.DMA((3, 2))],
        compiler_params=pltpu.CompilerParams(vmem_limit_bytes=3 * 2**20),
        cost_estimate=small_cost(),
        name="stage_columns",
    )(meta, in_hbm(vec), *after)


def fill_own(values, meta, after):
    rows, slots, size = values.shape[0] // 2, values.shape[1], values.shape[2]

    def kernel(meta, values, after, blocks, sem):
        for side in range(2):

            @pl.when(meta[0] == side)
            def _():
                run_copies(
                    [
                        pltpu.make_async_copy(
                            values.at[pl.ds(side * rows, rows)], blocks.at[:, pl.ds(side * slots, slots)], sem.at[side]
                        )
                    ]
                )

    return pl.pallas_call(
        kernel,
        out_shape=pltpu.VMEM((rows, 2 * slots, size, size), BF16),
        in_specs=[SCALARS, ANY, ANY],
        out_specs=RESIDENT,
        scratch_shapes=[pltpu.SemaphoreType.DMA((2,))],
        compiler_params=pltpu.CompilerParams(vmem_limit_bytes=4 * 2**20),
        cost_estimate=small_cost(),
        name="fill_own",
    )(meta, in_hbm(values), after)


def make_tables(cols, cols_other, counts, meta):
    slots, rows = cols.shape[0], cols.shape[1] // 2

    def kernel(meta, counts, cols, cols_other, tab, order):
        for low in range(2):
            place = jnp.where(meta[0] == low, cols[...], cols_other[...]) - meta[1]
            upper = lax.broadcasted_iota(jnp.int32, place.shape, 1) >= rows
            turned = jnp.where(place < rows, place + 2 * rows, jnp.where(place < 2 * rows, place, place - 2 * rows))
            tab[low * slots : (low + 1) * slots, :] = jnp.where(upper, turned, place + rows)
        for base in (0, rows):
            count = [counts[base + r] for r in range(rows)]
            rank = [jnp.int32(0)] * rows
            for i in range(rows):
                for j in range(i + 1, rows):
                    later = (count[j] > count[i]).astype(jnp.int32)
                    rank[i] += later
                    rank[j] += 1 - later
            for r in range(rows):
                order[base + rank[r]] = r

    return pl.pallas_call(
        kernel,
        out_shape=[
            jax.ShapeDtypeStruct((2 * slots, 2 * rows), jnp.int32),
            jax.ShapeDtypeStruct((2 * rows,), jnp.int32),
        ],
        in_specs=[SCALARS, SCALARS, RESIDENT, RESIDENT],
        out_specs=[RESIDENT, SCALARS],
        compiler_params=pltpu.CompilerParams(vmem_limit_bytes=2**20),
        cost_estimate=small_cost(),
        name="make_tables",
    )(meta, counts, cols, cols_other)


def together(*arrays):
    def kernel(*refs):
        del refs

    return pl.pallas_call(
        kernel,
        out_shape=[jax.ShapeDtypeStruct(x.shape, x.dtype) for x in arrays],
        in_specs=[ANY] * len(arrays),
        out_specs=[ANY] * len(arrays),
        input_output_aliases={n: n for n in range(len(arrays))},
        compiler_params=pltpu.CompilerParams(vmem_limit_bytes=2**20),
        cost_estimate=small_cost(),
        name="together",
    )(*arrays)


def product(label, other_half, tables, blocks, pieces, extras, outputs, scratch, emit, before=None, finish=None, aliases=(), after=()):
    rows, size, width = pieces[0][0].shape
    parts = len(pieces[0])
    columns = parts * width
    total_slots = blocks.shape[1]
    flat = [part for piece in pieces for part in piece]
    names = ["tab", "cnt", "order", "meta", "blocks_in"] + [f"piece{n}" for n in range(len(flat))]
    extras = {**extras, **{f"after{n}": x for n, x in enumerate(after)}}
    names += list(extras) + list(outputs) + ["field", "in_sems", "sems"] + list(scratch)

    def kernel(*refs):
        env = types.SimpleNamespace(**dict(zip(names, refs)))
        env.lay = env.meta[0]
        env.rows, env.half = rows, columns // 2
        env.blocks = getattr(env, "blocks", env.blocks_in)
        copies = [
            pltpu.make_async_copy(
                getattr(env, f"piece{n}"),
                env.field.at[pl.ds(n // parts * rows, rows), :, pl.ds(n % parts * width, width)],
                env.in_sems.at[n],
            )
            for n in range(len(flat))
        ]
        base = (1 - env.lay if other_half else env.lay) * rows
        now, later = before(env) if before else ([], [])
        start_all(copies + now + later)
        if hasattr(env, "fill"):
            env.fill()
        wait_all(copies + now)

        def some_rows(i, carry):
            picked = [env.order[base + i * TOGETHER + j] for j in range(TOGETHER)]
            counts = [env.cnt[base + r] for r in picked]
            used = (counts[0] + (GROUP - 1)) // GROUP
            for m in range(1, total_slots // GROUP + 1):

                @pl.when(used == m)
                def _():
                    for r, count in zip(picked, counts):
                        left, right = [], []
                        for k in range(m * GROUP):
                            block = env.blocks[r, k]
                            left.append(jnp.where(k < count, block, jnp.zeros_like(block)))
                            right.append(env.field[env.tab[k, base + r]])
                        emit(
                            env,
                            r,
                            jnp.dot(
                                jnp.concatenate(left, axis=1),
                                jnp.concatenate(right, axis=0),
                                preferred_element_type=F32,
                            ),
                        )

            if finish:
                for r in picked:
                    finish(env, r).start()
            return carry

        lax.fori_loop(0, rows // TOGETHER, some_rows, 0)
        if finish:

            def await_row(r, carry):
                finish(env, r).wait()
                return carry

            lax.fori_loop(0, rows, await_row, 0)
        wait_all(later)

    inputs = [in_vmem(blocks)] + flat + list(extras.values())
    result = pl.pallas_call(
        kernel,
        out_shape=[shape for shape, _ in outputs.values()],
        in_specs=[SCALARS] * 4 + [RESIDENT] + [ANY] * (len(inputs) - 1),
        out_specs=[spec for _, spec in outputs.values()],
        scratch_shapes=[
            pltpu.VMEM((len(pieces) * rows, size, columns), BF16),
            pltpu.SemaphoreType.DMA((len(flat),)),
            pltpu.SemaphoreType.DMA((4,)),
        ]
        + list(scratch.values()),
        input_output_aliases={names.index(i): list(outputs).index(o) for i, o in aliases},
        compiler_params=pltpu.CompilerParams(vmem_limit_bytes=10 * 2**20),
        cost_estimate=small_cost(),
        name=label,
    )(*tables, *inputs)
    return dict(zip(outputs, result))


def body(chips, values, cols, counts, vectors):
    rows = values.shape[0] // 2
    slots, size = values.shape[1], values.shape[2]
    columns = vectors.shape[1] // 2
    half = columns // 2
    lay = lax.axis_index("layer").astype(jnp.int32)
    start = lax.axis_index(("row", "col")).astype(jnp.int32) * 2 * rows
    up = [(chips + i, i + 1) for i in range(chips - 1)]
    across = up + [(b, a) for a, b in up]
    within = [(i, chips + i) for i in range(chips)] + [(chips + i, i) for i in range(chips)]
    along = [(i + 1, i) for i in range(chips - 1)] + [(chips + i, chips + i + 1) for i in range(chips - 1)]
    cross = lambda x: lax.ppermute(x, AXES, across)
    swap = lambda x: lax.ppermute(x, AXES, within)
    pass_on = lambda x: lax.ppermute(x, AXES, along)

    meta = jnp.stack([lay, start])
    vec = vectors.reshape(2 * rows, size, 2 * columns)
    other = swap(values)
    mine = list(stage_columns(vec, meta, True))
    halo = [cross(mine[q]) for q in range(2)]
    cols = cols.T
    cols_other = swap(cols)
    partner = list(stage_columns(vec, meta, False, [mine[0]]))
    blocks = fill_own(values, meta, mine[0])
    tab, order = make_tables(cols, cols_other, counts, meta)
    tables = (tab, counts, order, meta)

    wide, narrow = (rows, size, columns), (rows, size, half)
    held = lambda shape, dtype: (pltpu.VMEM(shape, dtype), RESIDENT)

    def halves(env, x):
        left, right = x[:, : env.half], x[:, env.half :]
        return jnp.where(env.lay == 0, left, right), jnp.where(env.lay == 0, right, left)

    def fill_other(env):
        def fill():
            for side in range(2):

                @pl.when(env.lay == side)
                def _():
                    run_copies(
                        [
                            pltpu.make_async_copy(
                                env.other.at[pl.ds(side * rows, rows)],
                                env.blocks.at[:, pl.ds((1 - side) * slots, slots)],
                                env.sems.at[side],
                            )
                        ]
                    )

        env.fill = fill
        return [], []

    def emit_first(env, r, total):
        env.keep[r], env.send[r] = halves(env, total)
        env.mine[r] = total.astype(BF16)

    first, first_other, pieces = [None] * 2, [None] * 2, [None] * 2
    for q in range(2):
        outputs = {"keep": held(narrow, F32), "send": held(narrow, F32), "mine": held(wide, BF16)}
        out = product(
            f"product_0_{q}",
            False,
            tables,
            blocks,
            ([halo[q]], [mine[q]], [partner[q]]),
            {"other": in_hbm(other)} if q == 0 else {},
            {"blocks": held(blocks.shape, BF16), **outputs} if q == 0 else outputs,
            {},
            emit_first,
            before=fill_other if q == 0 else None,
            aliases=[("blocks_in", "blocks")] if q == 0 else (),
        )
        blocks = out.get("blocks", blocks)
        first[q] = out["keep"]
        first_other[q] = swap(out["send"])
        swapped = swap(out["mine"])
        pieces[q] = ([cross(out["mine"])], [out["mine"]], [swapped])

    def fill_rest(env):
        copies = []
        for n, source in enumerate((env.values, env.other)):
            at = (env.lay if n == 0 else 1 - env.lay) * slots
            copies.append(
                pltpu.make_async_copy(
                    source.at[pl.ds((1 - env.lay) * rows, rows)], env.rest.at[:, pl.ds(at, slots)], env.sems.at[n]
                )
            )
        return [], copies

    def emit_second(env, r, total):
        keep, send = halves(env, total)
        env.keep[r], env.send[r] = keep.astype(BF16), send.astype(BF16)

    rest, second, far, near, second_other = None, [None] * 2, [None] * 2, [None] * 2, [None] * 2
    for q in range(2):
        outputs = {"keep": held(narrow, BF16), "send": held(narrow, BF16)}
        out = product(
            f"product_1_{q}",
            False,
            tables,
            blocks,
            pieces[q],
            {"values": in_hbm(values), "other": in_hbm(other)} if q == 0 else {},
            {"rest": held(blocks.shape, BF16), **outputs} if q == 0 else outputs,
            {},
            emit_second,
            before=fill_rest if q == 0 else None,
            after=[first[1], first_other[0]] if q == 0 else [first_other[1]],
        )
        rest = out.get("rest", rest)
        second[q] = out["keep"]
        second_other[q] = swap(out["send"])
        near[q] = cross(out["send"])
        far[q] = pass_on(out["keep"])

    far[0], near[0], second_other[0] = together(far[0], near[0], second_other[0])

    target_shape = (jax.ShapeDtypeStruct((2 * rows, size, columns), F32), ANY)

    def load_first(env):
        return [
            pltpu.make_async_copy(part, env.first_buf.at[:, :, pl.ds(q * half, half)], env.sems.at[q])
            for q, part in enumerate((env.first_0, env.first_1))
        ], []

    def emit_last(env, r, total):
        env.kept[r] = 1.5 * env.first_buf[r] - 0.5 * total

    target = None
    for other_half in (True, False):

        def finish_last(env, r, other_half=other_half):
            side = 1 - env.lay if other_half else env.lay
            return pltpu.make_async_copy(env.kept.at[r], env.target.at[side * rows + r], env.out_sems.at[r])

        extras = dict(zip(("first_0", "first_1"), first_other if other_half else first))
        if target is not None:
            extras["target_in"] = target
        target = product(
            "product_2",
            other_half,
            tables,
            rest if other_half else blocks,
            (far, second_other, second) if other_half else (near, second, second_other),
            extras,
            {"target": target_shape},
            {
                "kept": pltpu.VMEM(wide, F32),
                "first_buf": pltpu.VMEM(wide, F32),
                "out_sems": pltpu.SemaphoreType.DMA((rows,)),
            },
            emit_last,
            before=load_first,
            finish=finish_last,
            aliases=[("target_in", "target")] if target is not None else (),
        )["target"]
    return target.reshape(2 * rows * size, columns)


def solution(mesh):
    chips = mesh.shape["row"] * mesh.shape["col"]
    return jax.shard_map(
        functools.partial(body, chips),
        mesh=mesh,
        in_specs=(
            P(("row", "col"), "layer", None, None),
            P(("row", "col"), "layer"),
            P(("row", "col")),
            P(("row", "col"), None),
        ),
        out_specs=P(("row", "col"), "layer"),
        check_vma=False,
    )
```

```python
import functools
import types

import jax
import jax.numpy as jnp
from jax import lax
from jax.experimental import pallas as pl
from jax.experimental.pallas import tpu as pltpu
from jax.sharding import PartitionSpec as P

AXES = ("layer", "row", "col")
GROUP = 4
TOGETHER = 4
F32, BF16 = jnp.float32, jnp.bfloat16
ANY = pl.BlockSpec(memory_space=pl.ANY)
SCALARS = pl.BlockSpec(memory_space=pltpu.SMEM)
RESIDENT = pl.BlockSpec(memory_space=pltpu.VMEM)


def in_vmem(x):
    return pltpu.with_memory_space_constraint(x, pltpu.VMEM)


def in_hbm(x):
    return pltpu.with_memory_space_constraint(x, pltpu.HBM)


def start_all(copies):
    for copy in copies:
        copy.start()


def wait_all(copies):
    for copy in copies:
        copy.wait()


def run_copies(copies):
    start_all(copies)
    wait_all(copies)


def small_cost():
    return pl.CostEstimate(flops=0, bytes_accessed=1024, transcendentals=0)


def stage_columns(vec, meta, own, after=()):
    rows, size, columns = vec.shape[0] // 2, vec.shape[1], vec.shape[2] // 2
    half = columns // 2

    def kernel(meta, vec, *refs):
        left, right, whole, sems = refs[-4:]
        at = (meta[0] if own else 1 - meta[0]) * rows
        run_copies([pltpu.make_async_copy(vec.at[pl.ds(at, rows)], whole, sems.at[0, 0])])
        run_copies(
            [
                pltpu.make_async_copy(
                    whole.at[:, :, pl.ds((2 * h + piece) * half, half)],
                    out.at[:, :, pl.ds(h * half, half)],
                    sems.at[1 + piece, h],
                )
                for piece, out in enumerate((left, right))
                for h in range(2)
            ]
        )

    shape = (rows, size, columns)
    return pl.pallas_call(
        kernel,
        out_shape=[jax.ShapeDtypeStruct(shape, BF16) if own else pltpu.VMEM(shape, BF16)] * 2,
        in_specs=[SCALARS, ANY] + [ANY] * len(after),
        out_specs=[ANY if own else RESIDENT] * 2,
        scratch_shapes=[pltpu.VMEM((rows, size, 2 * columns), BF16), pltpu.SemaphoreType.DMA((3, 2))],
        compiler_params=pltpu.CompilerParams(vmem_limit_bytes=3 * 2**20),
        cost_estimate=small_cost(),
        name="stage_columns",
    )(meta, in_hbm(vec), *after)


def fill_own(values, counts, meta, after):
    rows, slots, size = values.shape[0] // 2, values.shape[1], values.shape[2]

    def kernel(meta, counts, values, after, blocks, order, sem):
        lay = meta[0]
        copy = pltpu.make_async_copy(
            values.at[pl.ds(lay * rows, rows)], blocks.at[:, pl.ds(lay * slots, slots)], sem.at[0]
        )
        copy.start()
        for base in (0, rows):
            count = [counts[base + r] for r in range(rows)]
            rank = [jnp.int32(0)] * rows
            for i in range(rows):
                for j in range(i + 1, rows):
                    later = (count[j] > count[i]).astype(jnp.int32)
                    rank[i] += later
                    rank[j] += 1 - later
            for r in range(rows):
                order[base + rank[r]] = r
        copy.wait()

    return pl.pallas_call(
        kernel,
        out_shape=[
            pltpu.VMEM((rows, 2 * slots, size, size), BF16),
            jax.ShapeDtypeStruct((2 * rows,), jnp.int32),
        ],
        in_specs=[SCALARS, SCALARS, ANY, ANY],
        out_specs=[RESIDENT, SCALARS],
        scratch_shapes=[pltpu.SemaphoreType.DMA((1,))],
        compiler_params=pltpu.CompilerParams(vmem_limit_bytes=4 * 2**20),
        cost_estimate=small_cost(),
        name="fill_own",
    )(meta, counts, in_hbm(values), after)


def make_table(cols, cols_other, meta):
    slots, rows = cols.shape[0], cols.shape[1] // 2

    def kernel(meta, cols, cols_other, tab):
        for low in range(2):
            place = jnp.where(meta[0] == low, cols[...], cols_other[...]) - meta[1]
            upper = lax.broadcasted_iota(jnp.int32, place.shape, 1) >= rows
            turned = jnp.where(place < rows, place + 2 * rows, jnp.where(place < 2 * rows, place, place - 2 * rows))
            tab[low * slots : (low + 1) * slots, :] = jnp.where(upper, turned, place + rows)

    return pl.pallas_call(
        kernel,
        out_shape=jax.ShapeDtypeStruct((2 * slots, 2 * rows), jnp.int32),
        in_specs=[SCALARS, RESIDENT, RESIDENT],
        out_specs=RESIDENT,
        compiler_params=pltpu.CompilerParams(vmem_limit_bytes=2**20),
        cost_estimate=small_cost(),
        name="make_table",
    )(meta, cols, cols_other)


def together(*arrays):
    def kernel(*refs):
        del refs

    return pl.pallas_call(
        kernel,
        out_shape=[jax.ShapeDtypeStruct(x.shape, x.dtype) for x in arrays],
        in_specs=[ANY] * len(arrays),
        out_specs=[ANY] * len(arrays),
        input_output_aliases={n: n for n in range(len(arrays))},
        compiler_params=pltpu.CompilerParams(vmem_limit_bytes=2**20),
        cost_estimate=small_cost(),
        name="together",
    )(*arrays)


def product(label, other_half, tables, blocks, pieces, extras, outputs, scratch, emit, before=None, arrive=None, finish=None, aliases=(), after=()):
    rows, size, width = pieces[0][0].shape
    parts = len(pieces[0])
    columns = parts * width
    total_slots = blocks.shape[1]
    flat = [part for piece in pieces for part in piece]
    names = ["tab", "cnt", "order", "meta", "blocks_in"] + [f"piece{n}" for n in range(len(flat))]
    extras = {**extras, **{f"after{n}": x for n, x in enumerate(after)}}
    names += list(extras) + list(outputs) + ["field", "in_sems", "sems"] + list(scratch)

    def kernel(*refs):
        env = types.SimpleNamespace(**dict(zip(names, refs)))
        env.lay = env.meta[0]
        env.rows, env.half = rows, columns // 2
        env.blocks = getattr(env, "blocks", env.blocks_in)
        copies = [
            pltpu.make_async_copy(
                getattr(env, f"piece{n}"),
                env.field.at[pl.ds(n // parts * rows, rows), :, pl.ds(n % parts * width, width)],
                env.in_sems.at[n],
            )
            for n in range(len(flat))
        ]
        base = (1 - env.lay if other_half else env.lay) * rows
        now, later = before(env) if before else ([], [])
        start_all(copies + now + later)
        wait_all(copies + now)

        def some_rows(i, carry):
            picked = [env.order[base + i * TOGETHER + j] for j in range(TOGETHER)]
            counts = [env.cnt[base + r] for r in picked]
            if arrive:
                for j, r in enumerate(picked):
                    arrive(env, i * TOGETHER + j, r).wait()
            used = (counts[0] + (GROUP - 1)) // GROUP
            for m in range(1, total_slots // GROUP + 1):

                @pl.when(used == m)
                def _():
                    for r, count in zip(picked, counts):
                        left, right = [], []
                        for k in range(m * GROUP):
                            block = env.blocks[r, k]
                            left.append(jnp.where(k < count, block, jnp.zeros_like(block)))
                            right.append(env.field[env.tab[k, base + r]])
                        emit(
                            env,
                            r,
                            jnp.dot(
                                jnp.concatenate(left, axis=1),
                                jnp.concatenate(right, axis=0),
                                preferred_element_type=F32,
                            ),
                        )

            if finish:
                for r in picked:
                    finish(env, r).start()
            return carry

        lax.fori_loop(0, rows // TOGETHER, some_rows, 0)
        if finish:

            def await_row(r, carry):
                finish(env, r).wait()
                return carry

            lax.fori_loop(0, rows, await_row, 0)
        wait_all(later)

    inputs = [in_vmem(blocks)] + flat + list(extras.values())
    result = pl.pallas_call(
        kernel,
        out_shape=[shape for shape, _ in outputs.values()],
        in_specs=[SCALARS] * 4
        + [RESIDENT]
        + [ANY] * (len(inputs) - 1),
        out_specs=[spec for _, spec in outputs.values()],
        scratch_shapes=[
            pltpu.VMEM((len(pieces) * rows, size, columns), BF16),
            pltpu.SemaphoreType.DMA((len(flat),)),
            pltpu.SemaphoreType.DMA((4,)),
        ]
        + list(scratch.values()),
        input_output_aliases={names.index(i): list(outputs).index(o) for i, o in aliases},
        compiler_params=pltpu.CompilerParams(vmem_limit_bytes=10 * 2**20),
        cost_estimate=small_cost(),
        name=label,
    )(*tables, *inputs)
    return dict(zip(outputs, result))


def body(chips, values, cols, counts, vectors):
    rows = values.shape[0] // 2
    slots, size = values.shape[1], values.shape[2]
    columns = vectors.shape[1] // 2
    half = columns // 2
    lay = lax.axis_index("layer").astype(jnp.int32)
    start = lax.axis_index(("row", "col")).astype(jnp.int32) * 2 * rows
    up = [(chips + i, i + 1) for i in range(chips - 1)]
    across = up + [(b, a) for a, b in up]
    within = [(i, chips + i) for i in range(chips)] + [(chips + i, i) for i in range(chips)]
    along = [(i + 1, i) for i in range(chips - 1)] + [(chips + i, chips + i + 1) for i in range(chips - 1)]
    cross = lambda x: lax.ppermute(x, AXES, across)
    swap = lambda x: lax.ppermute(x, AXES, within)
    pass_on = lambda x: lax.ppermute(x, AXES, along)

    meta = jnp.stack([lay, start])
    vec = vectors.reshape(2 * rows, size, 2 * columns)
    other = swap(values)
    mine = list(stage_columns(vec, meta, True))
    halo = [cross(mine[q]) for q in range(2)]
    cols = cols.T
    cols_other = swap(cols)
    partner = list(stage_columns(vec, meta, False, [mine[0]]))
    blocks, order = fill_own(values, counts, meta, mine[0])
    tables = (make_table(cols, cols_other, meta), counts, order, meta)

    wide, narrow = (rows, size, columns), (rows, size, half)
    held = lambda shape, dtype: (pltpu.VMEM(shape, dtype), RESIDENT)

    def halves(env, x):
        left, right = x[:, : env.half], x[:, env.half :]
        return jnp.where(env.lay == 0, left, right), jnp.where(env.lay == 0, right, left)

    def other_row(env, n, r):
        return pltpu.make_async_copy(
            env.other.at[env.lay * rows + r], env.blocks.at[r, pl.ds((1 - env.lay) * slots, slots)], env.row_sems.at[n]
        )

    def start_rows(env):
        for n in range(rows):
            other_row(env, n, env.order[env.lay * rows + n]).start()
        return [], []

    def emit_first(env, r, total):
        env.keep[r], env.send[r] = halves(env, total)
        env.mine[r] = total.astype(BF16)

    first, first_other, pieces = [None] * 2, [None] * 2, [None] * 2
    for q in range(2):
        outputs = {"keep": held(narrow, F32), "send": held(narrow, F32), "mine": held(wide, BF16)}
        out = product(
            f"product_0_{q}",
            False,
            tables,
            blocks,
            ([halo[q]], [mine[q]], [partner[q]]),
            {"other": in_hbm(other)} if q == 0 else {},
            {"blocks": held(blocks.shape, BF16), **outputs} if q == 0 else outputs,
            {"row_sems": pltpu.SemaphoreType.DMA((rows,))} if q == 0 else {},
            emit_first,
            before=start_rows if q == 0 else None,
            arrive=other_row if q == 0 else None,
            aliases=[("blocks_in", "blocks")] if q == 0 else (),
        )
        blocks = out.get("blocks", blocks)
        first[q] = out["keep"]
        first_other[q] = swap(out["send"])
        swapped = swap(out["mine"])
        pieces[q] = ([cross(out["mine"])], [out["mine"]], [swapped])

    def fill_rest(env):
        copies = []
        for n, source in enumerate((env.values, env.other)):
            at = (env.lay if n == 0 else 1 - env.lay) * slots
            copies.append(
                pltpu.make_async_copy(
                    source.at[pl.ds((1 - env.lay) * rows, rows)], env.rest.at[:, pl.ds(at, slots)], env.sems.at[n]
                )
            )
        return [], copies

    def emit_second(env, r, total):
        keep, send = halves(env, total)
        env.keep[r], env.send[r] = keep.astype(BF16), send.astype(BF16)

    rest, second, far, near, second_other = None, [None] * 2, [None] * 2, [None] * 2, [None] * 2
    for q in range(2):
        outputs = {"keep": held(narrow, BF16), "send": held(narrow, BF16)}
        out = product(
            f"product_1_{q}",
            False,
            tables,
            blocks,
            pieces[q],
            {"values": in_hbm(values), "other": in_hbm(other)} if q == 0 else {},
            {"rest": held(blocks.shape, BF16), **outputs} if q == 0 else outputs,
            {},
            emit_second,
            before=fill_rest if q == 0 else None,
            after=[first[1], first_other[0]] if q == 0 else [first_other[1]],
        )
        rest = out.get("rest", rest)
        second[q] = out["keep"]
        second_other[q] = swap(out["send"])
        near[q] = cross(out["send"])
        far[q] = pass_on(out["keep"])

    far[0], near[0], second_other[0] = together(far[0], near[0], second_other[0])

    target_shape = (jax.ShapeDtypeStruct((2 * rows, size, columns), F32), ANY)

    def load_first(env):
        return [
            pltpu.make_async_copy(part, env.first_buf.at[:, :, pl.ds(q * half, half)], env.sems.at[q])
            for q, part in enumerate((env.first_0, env.first_1))
        ], []

    def emit_last(env, r, total):
        env.kept[r] = 1.5 * env.first_buf[r] - 0.5 * total

    target = None
    for other_half in (True, False):

        def finish_last(env, r, other_half=other_half):
            side = 1 - env.lay if other_half else env.lay
            return pltpu.make_async_copy(env.kept.at[r], env.target.at[side * rows + r], env.out_sems.at[r])

        extras = dict(zip(("first_0", "first_1"), first_other if other_half else first))
        if target is not None:
            extras["target_in"] = target
        target = product(
            "product_2",
            other_half,
            tables,
            rest if other_half else blocks,
            (far, second_other, second) if other_half else (near, second, second_other),
            extras,
            {"target": target_shape},
            {
                "kept": pltpu.VMEM(wide, F32),
                "first_buf": pltpu.VMEM(wide, F32),
                "out_sems": pltpu.SemaphoreType.DMA((rows,)),
            },
            emit_last,
            before=load_first,
            finish=finish_last,
            aliases=[("target_in", "target")] if target is not None else (),
        )["target"]
    return target.reshape(2 * rows * size, columns)


def solution(mesh):
    chips = mesh.shape["row"] * mesh.shape["col"]
    return jax.shard_map(
        functools.partial(body, chips),
        mesh=mesh,
        in_specs=(
            P(("row", "col"), "layer", None, None),
            P(("row", "col"), "layer"),
            P(("row", "col")),
            P(("row", "col"), None),
        ),
        out_specs=P(("row", "col"), "layer"),
        check_vma=False,
    )
```

```python
import functools
import types

import jax
import jax.numpy as jnp
from jax import lax
from jax.experimental import pallas as pl
from jax.experimental.pallas import tpu as pltpu
from jax.sharding import PartitionSpec as P

AXES = ("layer", "row", "col")
GROUP = 4
TOGETHER = 4
F32, BF16 = jnp.float32, jnp.bfloat16
ANY = pl.BlockSpec(memory_space=pl.ANY)
SCALARS = pl.BlockSpec(memory_space=pltpu.SMEM)
RESIDENT = pl.BlockSpec(memory_space=pltpu.VMEM)


def in_vmem(x):
    return pltpu.with_memory_space_constraint(x, pltpu.VMEM)


def in_hbm(x):
    return pltpu.with_memory_space_constraint(x, pltpu.HBM)


def start_all(copies):
    for copy in copies:
        copy.start()


def wait_all(copies):
    for copy in copies:
        copy.wait()


def run_copies(copies):
    start_all(copies)
    wait_all(copies)


def small_cost():
    return pl.CostEstimate(flops=0, bytes_accessed=1024, transcendentals=0)


def stage_columns(vec, meta, own, after=()):
    rows, size, columns = vec.shape[0] // 2, vec.shape[1], vec.shape[2] // 2
    half = columns // 2
    share = 4

    def kernel(meta, vec, *refs):
        left, right, whole, load_sems, store_sems = refs[-5:]
        at = (meta[0] if own else 1 - meta[0]) * rows
        loads, stores = [], []
        for n in range(rows // share):
            part = pl.ds(n * share, share)
            loads.append(pltpu.make_async_copy(vec.at[pl.ds(at + n * share, share)], whole.at[part], load_sems.at[n]))
            stores.append(
                [
                    pltpu.make_async_copy(
                        whole.at[part, :, pl.ds((2 * h + piece) * half, half)],
                        out.at[part, :, pl.ds(h * half, half)],
                        store_sems.at[n, piece, h],
                    )
                    for piece, out in enumerate((left, right))
                    for h in range(2)
                ]
            )
        start_all(loads)
        for load, some in zip(loads, stores):
            load.wait()
            start_all(some)
        for some in stores:
            wait_all(some)

    shape = (rows, size, columns)
    return pl.pallas_call(
        kernel,
        out_shape=[jax.ShapeDtypeStruct(shape, BF16) if own else pltpu.VMEM(shape, BF16)] * 2,
        in_specs=[SCALARS, ANY] + [ANY] * len(after),
        out_specs=[ANY if own else RESIDENT] * 2,
        scratch_shapes=[
            pltpu.VMEM((rows, size, 2 * columns), BF16),
            pltpu.SemaphoreType.DMA((rows // share,)),
            pltpu.SemaphoreType.DMA((rows // share, 2, 2)),
        ],
        compiler_params=pltpu.CompilerParams(vmem_limit_bytes=3 * 2**20),
        cost_estimate=small_cost(),
        name="stage_columns",
    )(meta, in_hbm(vec), *after)


def fill_own(values, counts, meta, after):
    rows, slots, size = values.shape[0] // 2, values.shape[1], values.shape[2]

    def kernel(meta, counts, values, after, blocks, order, sem):
        lay = meta[0]
        copy = pltpu.make_async_copy(
            values.at[pl.ds(lay * rows, rows)], blocks.at[:, pl.ds(lay * slots, slots)], sem.at[0]
        )
        copy.start()
        for base in (0, rows):
            count = [counts[base + r] for r in range(rows)]
            rank = [jnp.int32(0)] * rows
            for i in range(rows):
                for j in range(i + 1, rows):
                    later = (count[j] > count[i]).astype(jnp.int32)
                    rank[i] += later
                    rank[j] += 1 - later
            for r in range(rows):
                order[base + rank[r]] = r
        copy.wait()

    return pl.pallas_call(
        kernel,
        out_shape=[
            pltpu.VMEM((rows, 2 * slots, size, size), BF16),
            jax.ShapeDtypeStruct((2 * rows,), jnp.int32),
        ],
        in_specs=[SCALARS, SCALARS, ANY, ANY],
        out_specs=[RESIDENT, SCALARS],
        scratch_shapes=[pltpu.SemaphoreType.DMA((1,))],
        compiler_params=pltpu.CompilerParams(vmem_limit_bytes=4 * 2**20),
        cost_estimate=small_cost(),
        name="fill_own",
    )(meta, counts, in_hbm(values), after)


def make_table(cols, cols_other, meta):
    slots, rows = cols.shape[0], cols.shape[1] // 2

    def kernel(meta, cols, cols_other, tab):
        for low in range(2):
            place = jnp.where(meta[0] == low, cols[...], cols_other[...]) - meta[1]
            upper = lax.broadcasted_iota(jnp.int32, place.shape, 1) >= rows
            turned = jnp.where(place < rows, place + 2 * rows, jnp.where(place < 2 * rows, place, place - 2 * rows))
            tab[low * slots : (low + 1) * slots, :] = jnp.where(upper, turned, place + rows)

    return pl.pallas_call(
        kernel,
        out_shape=jax.ShapeDtypeStruct((2 * slots, 2 * rows), jnp.int32),
        in_specs=[SCALARS, RESIDENT, RESIDENT],
        out_specs=RESIDENT,
        compiler_params=pltpu.CompilerParams(vmem_limit_bytes=2**20),
        cost_estimate=small_cost(),
        name="make_table",
    )(meta, cols, cols_other)


def together(*arrays):
    def kernel(*refs):
        del refs

    return pl.pallas_call(
        kernel,
        out_shape=[jax.ShapeDtypeStruct(x.shape, x.dtype) for x in arrays],
        in_specs=[ANY] * len(arrays),
        out_specs=[ANY] * len(arrays),
        input_output_aliases={n: n for n in range(len(arrays))},
        compiler_params=pltpu.CompilerParams(vmem_limit_bytes=2**20),
        cost_estimate=small_cost(),
        name="together",
    )(*arrays)


def product(label, other_half, tables, blocks, pieces, extras, outputs, scratch, emit, before=None, arrive=None, finish=None, aliases=(), after=()):
    rows, size, width = pieces[0][0].shape
    parts = len(pieces[0])
    columns = parts * width
    total_slots = blocks.shape[1]
    flat = [part for piece in pieces for part in piece]
    names = ["tab", "cnt", "order", "meta", "blocks_in"] + [f"piece{n}" for n in range(len(flat))]
    extras = {**extras, **{f"after{n}": x for n, x in enumerate(after)}}
    names += list(extras) + list(outputs) + ["field", "in_sems", "sems"] + list(scratch)

    def kernel(*refs):
        env = types.SimpleNamespace(**dict(zip(names, refs)))
        env.lay = env.meta[0]
        env.rows, env.half = rows, columns // 2
        env.blocks = getattr(env, "blocks", env.blocks_in)
        copies = [
            pltpu.make_async_copy(
                getattr(env, f"piece{n}"),
                env.field.at[pl.ds(n // parts * rows, rows), :, pl.ds(n % parts * width, width)],
                env.in_sems.at[n],
            )
            for n in range(len(flat))
        ]
        base = (1 - env.lay if other_half else env.lay) * rows
        now, later = before(env) if before else ([], [])
        start_all(copies + now + later)
        wait_all(copies + now)

        def some_rows(i, carry):
            picked = [env.order[base + i * TOGETHER + j] for j in range(TOGETHER)]
            counts = [env.cnt[base + r] for r in picked]
            if arrive:
                for j, r in enumerate(picked):
                    arrive(env, i * TOGETHER + j, r).wait()
            used = (counts[0] + (GROUP - 1)) // GROUP
            for m in range(1, total_slots // GROUP + 1):

                @pl.when(used == m)
                def _():
                    for r, count in zip(picked, counts):
                        left, right = [], []
                        for k in range(m * GROUP):
                            block = env.blocks[r, k]
                            left.append(jnp.where(k < count, block, jnp.zeros_like(block)))
                            right.append(env.field[env.tab[k, base + r]])
                        emit(
                            env,
                            r,
                            jnp.dot(
                                jnp.concatenate(left, axis=1),
                                jnp.concatenate(right, axis=0),
                                preferred_element_type=F32,
                            ),
                        )

            if finish:
                for r in picked:
                    finish(env, r).start()
            return carry

        lax.fori_loop(0, rows // TOGETHER, some_rows, 0)
        if finish:

            def await_row(r, carry):
                finish(env, r).wait()
                return carry

            lax.fori_loop(0, rows, await_row, 0)
        wait_all(later)

    inputs = [in_vmem(blocks)] + flat + list(extras.values())
    result = pl.pallas_call(
        kernel,
        out_shape=[shape for shape, _ in outputs.values()],
        in_specs=[SCALARS] * 4
        + [RESIDENT]
        + [ANY] * (len(inputs) - 1),
        out_specs=[spec for _, spec in outputs.values()],
        scratch_shapes=[
            pltpu.VMEM((len(pieces) * rows, size, columns), BF16),
            pltpu.SemaphoreType.DMA((len(flat),)),
            pltpu.SemaphoreType.DMA((4,)),
        ]
        + list(scratch.values()),
        input_output_aliases={names.index(i): list(outputs).index(o) for i, o in aliases},
        compiler_params=pltpu.CompilerParams(vmem_limit_bytes=10 * 2**20),
        cost_estimate=small_cost(),
        name=label,
    )(*tables, *inputs)
    return dict(zip(outputs, result))


def body(chips, values, cols, counts, vectors):
    rows = values.shape[0] // 2
    slots, size = values.shape[1], values.shape[2]
    columns = vectors.shape[1] // 2
    half = columns // 2
    lay = lax.axis_index("layer").astype(jnp.int32)
    start = lax.axis_index(("row", "col")).astype(jnp.int32) * 2 * rows
    up = [(chips + i, i + 1) for i in range(chips - 1)]
    across = up + [(b, a) for a, b in up]
    within = [(i, chips + i) for i in range(chips)] + [(chips + i, i) for i in range(chips)]
    along = [(i + 1, i) for i in range(chips - 1)] + [(chips + i, chips + i + 1) for i in range(chips - 1)]
    cross = lambda x: lax.ppermute(x, AXES, across)
    swap = lambda x: lax.ppermute(x, AXES, within)
    pass_on = lambda x: lax.ppermute(x, AXES, along)

    meta = jnp.stack([lay, start])
    vec = vectors.reshape(2 * rows, size, 2 * columns)
    other = swap(values)
    mine = list(stage_columns(vec, meta, True))
    halo = [cross(mine[q]) for q in range(2)]
    cols = cols.T
    cols_other = swap(cols)
    partner = list(stage_columns(vec, meta, False, [mine[0]]))
    blocks, order = fill_own(values, counts, meta, mine[0])
    tables = (make_table(cols, cols_other, meta), counts, order, meta)

    wide, narrow = (rows, size, columns), (rows, size, half)
    held = lambda shape, dtype: (pltpu.VMEM(shape, dtype), RESIDENT)

    def halves(env, x):
        left, right = x[:, : env.half], x[:, env.half :]
        return jnp.where(env.lay == 0, left, right), jnp.where(env.lay == 0, right, left)

    def other_row(env, n, r):
        return pltpu.make_async_copy(
            env.other.at[env.lay * rows + r], env.blocks.at[r, pl.ds((1 - env.lay) * slots, slots)], env.row_sems.at[n]
        )

    def start_rows(env):
        for n in range(rows):
            other_row(env, n, env.order[env.lay * rows + n]).start()
        return [], []

    def emit_first(env, r, total):
        env.keep[r], env.send[r] = halves(env, total)
        env.mine[r] = total.astype(BF16)

    first, first_other, pieces = [None] * 2, [None] * 2, [None] * 2
    for q in range(2):
        outputs = {"keep": held(narrow, F32), "send": held(narrow, F32), "mine": held(wide, BF16)}
        out = product(
            f"product_0_{q}",
            False,
            tables,
            blocks,
            ([halo[q]], [mine[q]], [partner[q]]),
            {"other": in_hbm(other)} if q == 0 else {},
            {"blocks": held(blocks.shape, BF16), **outputs} if q == 0 else outputs,
            {"row_sems": pltpu.SemaphoreType.DMA((rows,))} if q == 0 else {},
            emit_first,
            before=start_rows if q == 0 else None,
            arrive=other_row if q == 0 else None,
            aliases=[("blocks_in", "blocks")] if q == 0 else (),
        )
        blocks = out.get("blocks", blocks)
        first[q] = out["keep"]
        first_other[q] = swap(out["send"])
        swapped = swap(out["mine"])
        pieces[q] = ([cross(out["mine"])], [out["mine"]], [swapped])

    def fill_rest(env):
        copies = []
        for n, source in enumerate((env.values, env.other)):
            at = (env.lay if n == 0 else 1 - env.lay) * slots
            copies.append(
                pltpu.make_async_copy(
                    source.at[pl.ds((1 - env.lay) * rows, rows)], env.rest.at[:, pl.ds(at, slots)], env.sems.at[n]
                )
            )
        return [], copies

    def emit_second(env, r, total):
        keep, send = halves(env, total)
        env.keep[r], env.send[r] = keep.astype(BF16), send.astype(BF16)

    rest, second, far, near, second_other = None, [None] * 2, [None] * 2, [None] * 2, [None] * 2
    for q in range(2):
        outputs = {"keep": held(narrow, BF16), "send": held(narrow, BF16)}
        out = product(
            f"product_1_{q}",
            False,
            tables,
            blocks,
            pieces[q],
            {"values": in_hbm(values), "other": in_hbm(other)} if q == 0 else {},
            {"rest": held(blocks.shape, BF16), **outputs} if q == 0 else outputs,
            {},
            emit_second,
            before=fill_rest if q == 0 else None,
            after=[first[1], first_other[0]] if q == 0 else [first_other[1]],
        )
        rest = out.get("rest", rest)
        second[q] = out["keep"]
        second_other[q] = swap(out["send"])
        near[q] = cross(out["send"])
        far[q] = pass_on(out["keep"])

    near[0], far[0], second_other[0] = together(near[0], far[0], second_other[0])

    target_shape = (jax.ShapeDtypeStruct((2 * rows, size, columns), F32), ANY)

    def load_first(env):
        return [
            pltpu.make_async_copy(part, env.first_buf.at[:, :, pl.ds(q * half, half)], env.sems.at[q])
            for q, part in enumerate((env.first_0, env.first_1))
        ], []

    def emit_last(env, r, total):
        env.kept[r] = 1.5 * env.first_buf[r] - 0.5 * total

    target = None
    for other_half in (False, True):

        def finish_last(env, r, other_half=other_half):
            side = 1 - env.lay if other_half else env.lay
            return pltpu.make_async_copy(env.kept.at[r], env.target.at[side * rows + r], env.out_sems.at[r])

        extras = dict(zip(("first_0", "first_1"), first_other if other_half else first))
        if target is not None:
            extras["target_in"] = target
        target = product(
            "product_2",
            other_half,
            tables,
            rest if other_half else blocks,
            (far, second_other, second) if other_half else (near, second, second_other),
            extras,
            {"target": target_shape},
            {
                "kept": pltpu.VMEM(wide, F32),
                "first_buf": pltpu.VMEM(wide, F32),
                "out_sems": pltpu.SemaphoreType.DMA((rows,)),
            },
            emit_last,
            before=load_first,
            finish=finish_last,
            aliases=[("target_in", "target")] if target is not None else (),
        )["target"]
    return target.reshape(2 * rows * size, columns)


def solution(mesh):
    chips = mesh.shape["row"] * mesh.shape["col"]
    return jax.shard_map(
        functools.partial(body, chips),
        mesh=mesh,
        in_specs=(
            P(("row", "col"), "layer", None, None),
            P(("row", "col"), "layer"),
            P(("row", "col")),
            P(("row", "col"), None),
        ),
        out_specs=P(("row", "col"), "layer"),
        check_vma=False,
    )
```

```python
import functools
import types

import jax
import jax.numpy as jnp
from jax import lax
from jax.experimental import pallas as pl
from jax.experimental.pallas import tpu as pltpu
from jax.sharding import PartitionSpec as P

AXES = ("layer", "row", "col")
GROUP = 4
TOGETHER = 4
F32, BF16 = jnp.float32, jnp.bfloat16
ANY = pl.BlockSpec(memory_space=pl.ANY)
SCALARS = pl.BlockSpec(memory_space=pltpu.SMEM)
RESIDENT = pl.BlockSpec(memory_space=pltpu.VMEM)


def in_vmem(x):
    return pltpu.with_memory_space_constraint(x, pltpu.VMEM)


def in_hbm(x):
    return pltpu.with_memory_space_constraint(x, pltpu.HBM)


def start_all(copies):
    for copy in copies:
        copy.start()


def wait_all(copies):
    for copy in copies:
        copy.wait()


def run_copies(copies):
    start_all(copies)
    wait_all(copies)


def small_cost():
    return pl.CostEstimate(flops=0, bytes_accessed=1024, transcendentals=0)


def stage_columns(vec, meta, own, after=()):
    rows, size, columns = vec.shape[0] // 2, vec.shape[1], vec.shape[2] // 2
    half = columns // 2
    share = 4

    def kernel(meta, vec, *refs):
        left, right, whole, load_sems, store_sems = refs[-5:]
        at = (meta[0] if own else 1 - meta[0]) * rows
        loads, stores = [], []
        for n in range(rows // share):
            part = pl.ds(n * share, share)
            loads.append(pltpu.make_async_copy(vec.at[pl.ds(at + n * share, share)], whole.at[part], load_sems.at[n]))
            stores.append(
                [
                    pltpu.make_async_copy(
                        whole.at[part, :, pl.ds((2 * h + piece) * half, half)],
                        out.at[part, :, pl.ds(h * half, half)],
                        store_sems.at[n, piece, h],
                    )
                    for piece, out in enumerate((left, right))
                    for h in range(2)
                ]
            )
        start_all(loads)
        for load, some in zip(loads, stores):
            load.wait()
            start_all(some)
        for some in stores:
            wait_all(some)

    shape = (rows, size, columns)
    return pl.pallas_call(
        kernel,
        out_shape=[jax.ShapeDtypeStruct(shape, BF16) if own else pltpu.VMEM(shape, BF16)] * 2,
        in_specs=[SCALARS, ANY] + [ANY] * len(after),
        out_specs=[ANY if own else RESIDENT] * 2,
        scratch_shapes=[
            pltpu.VMEM((rows, size, 2 * columns), BF16),
            pltpu.SemaphoreType.DMA((rows // share,)),
            pltpu.SemaphoreType.DMA((rows // share, 2, 2)),
        ],
        compiler_params=pltpu.CompilerParams(vmem_limit_bytes=3 * 2**20),
        cost_estimate=small_cost(),
        name="stage_columns",
    )(meta, in_hbm(vec), *after)


def fill_own(values, counts, meta, after):
    rows, slots, size = values.shape[0] // 2, values.shape[1], values.shape[2]

    def kernel(meta, counts, values, after, blocks, order, sem):
        lay = meta[0]
        copy = pltpu.make_async_copy(
            values.at[pl.ds(lay * rows, rows)], blocks.at[:, pl.ds(lay * slots, slots)], sem.at[0]
        )
        copy.start()
        for base in (0, rows):
            count = [counts[base + r] for r in range(rows)]
            rank = [jnp.int32(0)] * rows
            for i in range(rows):
                for j in range(i + 1, rows):
                    later = (count[j] > count[i]).astype(jnp.int32)
                    rank[i] += later
                    rank[j] += 1 - later
            for r in range(rows):
                order[base + rank[r]] = r
        copy.wait()

    return pl.pallas_call(
        kernel,
        out_shape=[
            pltpu.VMEM((rows, 2 * slots, size, size), BF16),
            jax.ShapeDtypeStruct((2 * rows,), jnp.int32),
        ],
        in_specs=[SCALARS, SCALARS, ANY, ANY],
        out_specs=[RESIDENT, SCALARS],
        scratch_shapes=[pltpu.SemaphoreType.DMA((1,))],
        compiler_params=pltpu.CompilerParams(vmem_limit_bytes=4 * 2**20),
        cost_estimate=small_cost(),
        name="fill_own",
    )(meta, counts, in_hbm(values), after)


def make_table(cols, cols_other, counts, meta):
    slots, rows = cols.shape[0], cols.shape[1] // 2
    total = 2 * slots

    def kernel(meta, counts, cols, cols_other, tab, held):
        for low in range(2):
            place = jnp.where(meta[0] == low, cols[...], cols_other[...]) - meta[1]
            upper = lax.broadcasted_iota(jnp.int32, place.shape, 1) >= rows
            turned = jnp.where(place < rows, place + 2 * rows, jnp.where(place < 2 * rows, place, place - 2 * rows))
            held[low * slots : (low + 1) * slots, :] = jnp.where(upper, turned, place + rows)
        place = held[...]
        slot = lax.broadcasted_iota(jnp.int32, place.shape, 0)
        lane = lax.broadcasted_iota(jnp.int32, place.shape, 1)
        count = jnp.zeros_like(place)
        for r in range(2 * rows):
            count = jnp.where(lane == r, counts[r], count)
        kind = jnp.where(slot >= count, 2, jnp.where(place < rows, 1, 0))
        held[...] = kind
        at = jnp.zeros_like(place)
        for k in range(total):
            other = held[k : k + 1, :]
            ahead = jnp.logical_or(other < kind, jnp.logical_and(other == kind, k < slot))
            at = at + ahead.astype(jnp.int32)
        tab[0:total, :] = place
        held[...] = at
        places, numbers = jnp.zeros_like(place), jnp.zeros_like(place)
        for k in range(total):
            here = held[k : k + 1, :] == slot
            places = jnp.where(here, tab[k : k + 1, :], places)
            numbers = jnp.where(here, k, numbers)
        tab[total : 2 * total, :] = places
        tab[2 * total : 3 * total, :] = numbers
        near = jnp.sum((kind == 0).astype(jnp.int32), axis=0, keepdims=True)
        tab[3 * total : 3 * total + 8, :] = jnp.broadcast_to(near, (8, 2 * rows))

    return pl.pallas_call(
        kernel,
        out_shape=jax.ShapeDtypeStruct((3 * total + 8, 2 * rows), jnp.int32),
        in_specs=[SCALARS, SCALARS, RESIDENT, RESIDENT],
        out_specs=RESIDENT,
        scratch_shapes=[pltpu.VMEM((total, 2 * rows), jnp.int32)],
        compiler_params=pltpu.CompilerParams(vmem_limit_bytes=2**20),
        cost_estimate=small_cost(),
        name="make_table",
    )(meta, counts, cols, cols_other)


def together(*arrays):
    def kernel(*refs):
        del refs

    return pl.pallas_call(
        kernel,
        out_shape=[jax.ShapeDtypeStruct(x.shape, x.dtype) for x in arrays],
        in_specs=[ANY] * len(arrays),
        out_specs=[ANY] * len(arrays),
        input_output_aliases={n: n for n in range(len(arrays))},
        compiler_params=pltpu.CompilerParams(vmem_limit_bytes=2**20),
        cost_estimate=small_cost(),
        name="together",
    )(*arrays)


def product(label, other_half, tables, blocks, pieces, extras, outputs, scratch, emit, before=None, arrive=None, finish=None, aliases=(), after=(), part=None):
    rows, size, width = pieces[0][0].shape
    parts = len(pieces[0])
    columns = parts * width
    total_slots = blocks.shape[1]
    flat = [part for piece in pieces for part in piece]
    names = ["tab", "cnt", "order", "meta", "blocks_in"] + [f"piece{n}" for n in range(len(flat))]
    extras = {**extras, **{f"after{n}": x for n, x in enumerate(after)}}
    names += list(extras) + list(outputs) + ["field", "in_sems", "sems"] + list(scratch)

    def kernel(*refs):
        env = types.SimpleNamespace(**dict(zip(names, refs)))
        env.lay = env.meta[0]
        env.rows, env.half = rows, columns // 2
        env.blocks = getattr(env, "blocks", env.blocks_in)
        copies = [
            pltpu.make_async_copy(
                getattr(env, f"piece{n}"),
                env.field.at[pl.ds(n // parts * rows, rows), :, pl.ds(n % parts * width, width)],
                env.in_sems.at[n],
            )
            for n in range(len(flat))
        ]
        base = (1 - env.lay if other_half else env.lay) * rows
        now, later = before(env) if before else ([], [])
        start_all(copies + now + later)
        wait_all(copies + now)

        def some_rows(i, carry):
            if part == "halo":
                picked = [i * TOGETHER + j for j in range(TOGETHER)]
            else:
                picked = [env.order[base + i * TOGETHER + j] for j in range(TOGETHER)]
            counts = [env.cnt[base + r] for r in picked]
            if arrive:
                for j, r in enumerate(picked):
                    arrive(env, i * TOGETHER + j, r).wait()
            most, first = counts[0], [0] * TOGETHER
            if part:
                inner = [env.tab[3 * total_slots, base + r] for r in picked]
                if part == "halo":
                    first, counts = inner, [count - n for count, n in zip(counts, inner)]
                else:
                    counts = inner
                most = functools.reduce(jnp.maximum, counts)
            used = (most + (GROUP - 1)) // GROUP
            if part:

                @pl.when(used == 0)
                def _():
                    for r in picked:
                        emit(env, r, jnp.zeros((size, columns), F32))

            for m in range(1, total_slots // GROUP + 1):

                @pl.when(used == m)
                def _():
                    for r, count, begin in zip(picked, counts, first):
                        left, right = [], []
                        for k in range(m * GROUP):
                            number, place = k, env.tab[k, base + r] if not part else None
                            if part:
                                n = jnp.minimum(begin + k, total_slots - 1)
                                number = env.tab[2 * total_slots + n, base + r]
                                place = env.tab[total_slots + n, base + r]
                                place = jnp.clip(place if part == "halo" else place - rows, 0, len(pieces) * rows - 1)
                            block = env.blocks[r, number]
                            left.append(jnp.where(k < count, block, jnp.zeros_like(block)))
                            right.append(env.field[place])
                        emit(
                            env,
                            r,
                            jnp.dot(
                                jnp.concatenate(left, axis=1),
                                jnp.concatenate(right, axis=0),
                                preferred_element_type=F32,
                            ),
                        )

            if finish:
                for r in picked:
                    finish(env, r).start()
            return carry

        lax.fori_loop(0, rows // TOGETHER, some_rows, 0)
        if finish:

            def await_row(r, carry):
                finish(env, r).wait()
                return carry

            lax.fori_loop(0, rows, await_row, 0)
        wait_all(later)

    inputs = [in_vmem(blocks)] + flat + list(extras.values())
    result = pl.pallas_call(
        kernel,
        out_shape=[shape for shape, _ in outputs.values()],
        in_specs=[SCALARS] * 4
        + [RESIDENT]
        + [ANY] * (len(inputs) - 1),
        out_specs=[spec for _, spec in outputs.values()],
        scratch_shapes=[
            pltpu.VMEM((len(pieces) * rows, size, columns), BF16),
            pltpu.SemaphoreType.DMA((len(flat),)),
            pltpu.SemaphoreType.DMA((4,)),
        ]
        + list(scratch.values()),
        input_output_aliases={names.index(i): list(outputs).index(o) for i, o in aliases},
        compiler_params=pltpu.CompilerParams(vmem_limit_bytes=10 * 2**20),
        cost_estimate=small_cost(),
        name=label,
    )(*tables, *inputs)
    return dict(zip(outputs, result))


def body(chips, values, cols, counts, vectors):
    rows = values.shape[0] // 2
    slots, size = values.shape[1], values.shape[2]
    columns = vectors.shape[1] // 2
    half = columns // 2
    lay = lax.axis_index("layer").astype(jnp.int32)
    start = lax.axis_index(("row", "col")).astype(jnp.int32) * 2 * rows
    up = [(chips + i, i + 1) for i in range(chips - 1)]
    across = up + [(b, a) for a, b in up]
    within = [(i, chips + i) for i in range(chips)] + [(chips + i, i) for i in range(chips)]
    along = [(i + 1, i) for i in range(chips - 1)] + [(chips + i, chips + i + 1) for i in range(chips - 1)]
    cross = lambda x: lax.ppermute(x, AXES, across)
    swap = lambda x: lax.ppermute(x, AXES, within)
    pass_on = lambda x: lax.ppermute(x, AXES, along)

    meta = jnp.stack([lay, start])
    vec = vectors.reshape(2 * rows, size, 2 * columns)
    other = swap(values)
    mine = list(stage_columns(vec, meta, True))
    halo = [cross(mine[q]) for q in range(2)]
    cols = cols.T
    cols_other = swap(cols)
    partner = list(stage_columns(vec, meta, False, [mine[0]]))
    blocks, order = fill_own(values, counts, meta, mine[0])
    tables = (make_table(cols, cols_other, counts, meta), counts, order, meta)

    wide, narrow = (rows, size, columns), (rows, size, half)
    held = lambda shape, dtype: (pltpu.VMEM(shape, dtype), RESIDENT)

    def halves(env, x):
        left, right = x[:, : env.half], x[:, env.half :]
        return jnp.where(env.lay == 0, left, right), jnp.where(env.lay == 0, right, left)

    def other_row(env, n, r):
        return pltpu.make_async_copy(
            env.other.at[env.lay * rows + r], env.blocks.at[r, pl.ds((1 - env.lay) * slots, slots)], env.row_sems.at[n]
        )

    def start_rows(env):
        for n in range(rows):
            other_row(env, n, env.order[env.lay * rows + n]).start()
        return [], []

    def emit_first(env, r, total):
        env.keep[r], env.send[r] = halves(env, total)
        env.mine[r] = total.astype(BF16)

    first, first_other, pieces = [None] * 2, [None] * 2, [None] * 2
    for q in range(2):
        outputs = {"keep": held(narrow, F32), "send": held(narrow, F32), "mine": held(wide, BF16)}
        out = product(
            f"product_0_{q}",
            False,
            tables,
            blocks,
            ([halo[q]], [mine[q]], [partner[q]]),
            {"other": in_hbm(other)} if q == 0 else {},
            {"blocks": held(blocks.shape, BF16), **outputs} if q == 0 else outputs,
            {"row_sems": pltpu.SemaphoreType.DMA((rows,))} if q == 0 else {},
            emit_first,
            before=start_rows if q == 0 else None,
            arrive=other_row if q == 0 else None,
            aliases=[("blocks_in", "blocks")] if q == 0 else (),
        )
        blocks = out.get("blocks", blocks)
        first[q] = out["keep"]
        first_other[q] = swap(out["send"])
        swapped = swap(out["mine"])
        pieces[q] = ([cross(out["mine"])], [out["mine"]], [swapped])

    def fill_rest(env):
        copies = []
        for n, source in enumerate((env.values, env.other)):
            at = (env.lay if n == 0 else 1 - env.lay) * slots
            copies.append(
                pltpu.make_async_copy(
                    source.at[pl.ds((1 - env.lay) * rows, rows)], env.rest.at[:, pl.ds(at, slots)], env.sems.at[2 + n]
                )
            )
        return copies

    def emit_second(env, r, total):
        keep, send = halves(env, total)
        env.keep[r], env.send[r] = keep.astype(BF16), send.astype(BF16)

    second, far, near, second_other = [None] * 2, [None] * 2, [None] * 2, [None] * 2
    for q in range(2):
        out = product(
            f"product_1_{q}",
            False,
            tables,
            blocks,
            pieces[q],
            {},
            {"keep": held(narrow, BF16), "send": held(narrow, BF16)},
            {},
            emit_second,
            after=[first[1], first_other[0]] if q == 0 else [first_other[1]],
        )
        second[q] = out["keep"]
        second_other[q] = swap(out["send"])
        near[q] = cross(out["send"])
        far[q] = pass_on(out["keep"])

    near[0], far[0], second_other[0] = together(near[0], far[0], second_other[0])

    target_shape = (jax.ShapeDtypeStruct((2 * rows, size, columns), F32), ANY)

    def load_first(env):
        return [
            pltpu.make_async_copy(part, env.first_buf.at[:, :, pl.ds(q * half, half)], env.sems.at[q])
            for q, part in enumerate((env.first_0, env.first_1))
        ], []

    def emit_last(env, r, total):
        env.kept[r] = 1.5 * env.first_buf[r] - 0.5 * total

    def emit_partial(env, r, total):
        env.partial[r] = 1.5 * env.first_buf[r] - 0.5 * total

    def load_partial(env):
        return [pltpu.make_async_copy(env.partial, env.first_buf, env.sems.at[0])], []

    def emit_rest(env, r, total):
        env.kept[r] = env.first_buf[r] - 0.5 * total

    def finish_half(other_half):
        def finish_last(env, r):
            side = 1 - env.lay if other_half else env.lay
            return pltpu.make_async_copy(env.kept.at[r], env.target.at[side * rows + r], env.out_sems.at[r])

        return finish_last

    buffers = {
        "kept": pltpu.VMEM(wide, F32),
        "first_buf": pltpu.VMEM(wide, F32),
        "out_sems": pltpu.SemaphoreType.DMA((rows,)),
    }
    out = product(
        "product_2_inner",
        False,
        tables,
        blocks,
        (second, second_other),
        {**dict(zip(("first_0", "first_1"), first)), "values": in_hbm(values), "other": in_hbm(other)},
        {"partial": held(wide, F32), "rest": held(blocks.shape, BF16)},
        {"first_buf": pltpu.VMEM(wide, F32)},
        emit_partial,
        before=lambda env: (load_first(env)[0], fill_rest(env)),
        part="main",
    )
    partial, rest = out["partial"], out["rest"]
    target = product(
        "product_2_halo",
        False,
        tables,
        blocks,
        (near,),
        {"partial": partial},
        {"target": target_shape},
        buffers,
        emit_rest,
        before=load_partial,
        finish=finish_half(False),
        part="halo",
    )["target"]
    target = product(
        "product_2_other",
        True,
        tables,
        rest,
        (far, second_other, second),
        {**dict(zip(("first_0", "first_1"), first_other)), "target_in": target},
        {"target": target_shape},
        buffers,
        emit_last,
        before=load_first,
        finish=finish_half(True),
        aliases=[("target_in", "target")],
    )["target"]
    return target.reshape(2 * rows * size, columns)


def solution(mesh):
    chips = mesh.shape["row"] * mesh.shape["col"]
    return jax.shard_map(
        functools.partial(body, chips),
        mesh=mesh,
        in_specs=(
            P(("row", "col"), "layer", None, None),
            P(("row", "col"), "layer"),
            P(("row", "col")),
            P(("row", "col"), None),
        ),
        out_specs=P(("row", "col"), "layer"),
        check_vma=False,
    )
```

```python
import functools
import types

import jax
import jax.numpy as jnp
from jax import lax
from jax.experimental import pallas as pl
from jax.experimental.pallas import tpu as pltpu
from jax.sharding import PartitionSpec as P

AXES = ("layer", "row", "col")
GROUP = 4
TOGETHER = 4
F32, BF16 = jnp.float32, jnp.bfloat16
ANY = pl.BlockSpec(memory_space=pl.ANY)
SCALARS = pl.BlockSpec(memory_space=pltpu.SMEM)
RESIDENT = pl.BlockSpec(memory_space=pltpu.VMEM)


def in_vmem(x):
    return pltpu.with_memory_space_constraint(x, pltpu.VMEM)


def in_hbm(x):
    return pltpu.with_memory_space_constraint(x, pltpu.HBM)


def start_all(copies):
    for copy in copies:
        copy.start()


def wait_all(copies):
    for copy in copies:
        copy.wait()


def run_copies(copies):
    start_all(copies)
    wait_all(copies)


def small_cost():
    return pl.CostEstimate(flops=0, bytes_accessed=1024, transcendentals=0)


def stage_columns(vec, meta, own, after=()):
    rows, size, columns = vec.shape[0] // 2, vec.shape[1], vec.shape[2] // 2
    half = columns // 2
    share = 4

    def kernel(meta, vec, *refs):
        left, right, whole, load_sems, store_sems = refs[-5:]
        at = (meta[0] if own else 1 - meta[0]) * rows
        loads, stores = [], []
        for n in range(rows // share):
            part = pl.ds(n * share, share)
            loads.append(pltpu.make_async_copy(vec.at[pl.ds(at + n * share, share)], whole.at[part], load_sems.at[n]))
            stores.append(
                [
                    pltpu.make_async_copy(
                        whole.at[part, :, pl.ds((2 * h + piece) * half, half)],
                        out.at[part, :, pl.ds(h * half, half)],
                        store_sems.at[n, piece, h],
                    )
                    for piece, out in enumerate((left, right))
                    for h in range(2)
                ]
            )
        start_all(loads)
        for load, some in zip(loads, stores):
            load.wait()
            start_all(some)
        for some in stores:
            wait_all(some)

    shape = (rows, size, columns)
    return pl.pallas_call(
        kernel,
        out_shape=[jax.ShapeDtypeStruct(shape, BF16) if own else pltpu.VMEM(shape, BF16)] * 2,
        in_specs=[SCALARS, ANY] + [ANY] * len(after),
        out_specs=[ANY if own else RESIDENT] * 2,
        scratch_shapes=[
            pltpu.VMEM((rows, size, 2 * columns), BF16),
            pltpu.SemaphoreType.DMA((rows // share,)),
            pltpu.SemaphoreType.DMA((rows // share, 2, 2)),
        ],
        compiler_params=pltpu.CompilerParams(vmem_limit_bytes=3 * 2**20),
        cost_estimate=small_cost(),
        name="stage_columns",
    )(meta, in_hbm(vec), *after)


def fill_own(values, counts, meta, after):
    rows, slots, size = values.shape[0] // 2, values.shape[1], values.shape[2]

    def kernel(meta, counts, values, after, blocks, order, sem):
        lay = meta[0]
        copy = pltpu.make_async_copy(
            values.at[pl.ds(lay * rows, rows)], blocks.at[:, pl.ds(lay * slots, slots)], sem.at[0]
        )
        copy.start()
        for base in (0, rows):
            count = [counts[base + r] for r in range(rows)]
            rank = [jnp.int32(0)] * rows
            for i in range(rows):
                for j in range(i + 1, rows):
                    later = (count[j] > count[i]).astype(jnp.int32)
                    rank[i] += later
                    rank[j] += 1 - later
            for r in range(rows):
                order[base + rank[r]] = r
        copy.wait()

    return pl.pallas_call(
        kernel,
        out_shape=[
            pltpu.VMEM((rows, 2 * slots, size, size), BF16),
            jax.ShapeDtypeStruct((2 * rows,), jnp.int32),
        ],
        in_specs=[SCALARS, SCALARS, ANY, ANY],
        out_specs=[RESIDENT, SCALARS],
        scratch_shapes=[pltpu.SemaphoreType.DMA((1,))],
        compiler_params=pltpu.CompilerParams(vmem_limit_bytes=4 * 2**20),
        cost_estimate=small_cost(),
        name="fill_own",
    )(meta, counts, in_hbm(values), after)


def make_table(cols, cols_other, meta):
    slots, rows = cols.shape[0], cols.shape[1] // 2

    def kernel(meta, cols, cols_other, tab):
        for low in range(2):
            place = jnp.where(meta[0] == low, cols[...], cols_other[...]) - meta[1]
            upper = lax.broadcasted_iota(jnp.int32, place.shape, 1) >= rows
            turned = jnp.where(place < rows, place + 2 * rows, jnp.where(place < 2 * rows, place, place - 2 * rows))
            tab[low * slots : (low + 1) * slots, :] = jnp.where(upper, turned, place + rows)

    return pl.pallas_call(
        kernel,
        out_shape=jax.ShapeDtypeStruct((2 * slots, 2 * rows), jnp.int32),
        in_specs=[SCALARS, RESIDENT, RESIDENT],
        out_specs=RESIDENT,
        compiler_params=pltpu.CompilerParams(vmem_limit_bytes=2**20),
        cost_estimate=small_cost(),
        name="make_table",
    )(meta, cols, cols_other)


def together(*arrays):
    def kernel(*refs):
        del refs

    return pl.pallas_call(
        kernel,
        out_shape=[jax.ShapeDtypeStruct(x.shape, x.dtype) for x in arrays],
        in_specs=[ANY] * len(arrays),
        out_specs=[ANY] * len(arrays),
        input_output_aliases={n: n for n in range(len(arrays))},
        compiler_params=pltpu.CompilerParams(vmem_limit_bytes=2**20),
        cost_estimate=small_cost(),
        name="together",
    )(*arrays)


def product(label, other_half, tables, blocks, pieces, extras, outputs, scratch, emit, before=None, arrive=None, finish=None, aliases=(), after=()):
    rows, size, width = pieces[0][0].shape
    parts = len(pieces[0])
    columns = parts * width
    total_slots = blocks.shape[1]
    flat = [part for piece in pieces for part in piece]
    names = ["tab", "cnt", "order", "meta", "blocks_in"] + [f"piece{n}" for n in range(len(flat))]
    extras = {**extras, **{f"after{n}": x for n, x in enumerate(after)}}
    names += list(extras) + list(outputs) + ["field", "in_sems", "sems"] + list(scratch)

    def kernel(*refs):
        env = types.SimpleNamespace(**dict(zip(names, refs)))
        env.lay = env.meta[0]
        env.rows, env.half = rows, columns // 2
        env.blocks = getattr(env, "blocks", env.blocks_in)
        copies = [
            pltpu.make_async_copy(
                getattr(env, f"piece{n}"),
                env.field.at[pl.ds(n // parts * rows, rows), :, pl.ds(n % parts * width, width)],
                env.in_sems.at[n],
            )
            for n in range(len(flat))
        ]
        base = (1 - env.lay if other_half else env.lay) * rows
        now, later = before(env) if before else ([], [])
        start_all(copies + now + later)
        wait_all(copies + now)

        def some_rows(i, carry):
            picked = [env.order[base + i * TOGETHER + j] for j in range(TOGETHER)]
            counts = [env.cnt[base + r] for r in picked]
            if arrive:
                for j, r in enumerate(picked):
                    arrive(env, i * TOGETHER + j, r).wait()
            used = (counts[0] + (GROUP - 1)) // GROUP
            for m in range(1, total_slots // GROUP + 1):

                @pl.when(used == m)
                def _():
                    for r, count in zip(picked, counts):
                        left, right = [], []
                        for k in range(m * GROUP):
                            block = env.blocks[r, k]
                            left.append(jnp.where(k < count, block, jnp.zeros_like(block)))
                            right.append(env.field[env.tab[k, base + r]])
                        emit(
                            env,
                            r,
                            jnp.dot(
                                jnp.concatenate(left, axis=1),
                                jnp.concatenate(right, axis=0),
                                preferred_element_type=F32,
                            ),
                        )

            if finish:
                for r in picked:
                    finish(env, r).start()
            return carry

        lax.fori_loop(0, rows // TOGETHER, some_rows, 0)
        if finish:

            def await_row(r, carry):
                finish(env, r).wait()
                return carry

            lax.fori_loop(0, rows, await_row, 0)
        wait_all(later)

    inputs = [in_vmem(blocks)] + flat + list(extras.values())
    result = pl.pallas_call(
        kernel,
        out_shape=[shape for shape, _ in outputs.values()],
        in_specs=[SCALARS] * 4
        + [RESIDENT]
        + [ANY] * (len(inputs) - 1),
        out_specs=[spec for _, spec in outputs.values()],
        scratch_shapes=[
            pltpu.VMEM((len(pieces) * rows, size, columns), BF16),
            pltpu.SemaphoreType.DMA((len(flat),)),
            pltpu.SemaphoreType.DMA((4,)),
        ]
        + list(scratch.values()),
        input_output_aliases={names.index(i): list(outputs).index(o) for i, o in aliases},
        compiler_params=pltpu.CompilerParams(vmem_limit_bytes=10 * 2**20),
        cost_estimate=small_cost(),
        name=label,
    )(*tables, *inputs)
    return dict(zip(outputs, result))


def body(chips, values, cols, counts, vectors):
    rows = values.shape[0] // 2
    slots, size = values.shape[1], values.shape[2]
    columns = vectors.shape[1] // 2
    half = columns // 2
    lay = lax.axis_index("layer").astype(jnp.int32)
    start = lax.axis_index(("row", "col")).astype(jnp.int32) * 2 * rows
    up = [(chips + i, i + 1) for i in range(chips - 1)]
    across = up + [(b, a) for a, b in up]
    within = [(i, chips + i) for i in range(chips)] + [(chips + i, i) for i in range(chips)]
    along = [(i + 1, i) for i in range(chips - 1)] + [(chips + i, chips + i + 1) for i in range(chips - 1)]
    cross = lambda x: lax.ppermute(x, AXES, across)
    swap = lambda x: lax.ppermute(x, AXES, within)
    pass_on = lambda x: lax.ppermute(x, AXES, along)

    meta = jnp.stack([lay, start])
    vec = vectors.reshape(2 * rows, size, 2 * columns)
    other = swap(values)
    mine = list(stage_columns(vec, meta, True))
    halo = [cross(mine[q]) for q in range(2)]
    cols = cols.T
    cols_other = swap(cols)
    partner = list(stage_columns(vec, meta, False, [mine[0]]))
    blocks, order = fill_own(values, counts, meta, mine[0])
    tables = (make_table(cols, cols_other, meta), counts, order, meta)

    wide, narrow = (rows, size, columns), (rows, size, half)
    held = lambda shape, dtype: (pltpu.VMEM(shape, dtype), RESIDENT)

    def halves(env, x):
        left, right = x[:, : env.half], x[:, env.half :]
        return jnp.where(env.lay == 0, left, right), jnp.where(env.lay == 0, right, left)

    def other_row(env, n, r):
        return pltpu.make_async_copy(
            env.other.at[env.lay * rows + r], env.blocks.at[r, pl.ds((1 - env.lay) * slots, slots)], env.row_sems.at[n]
        )

    def start_rows(env):
        for n in range(rows):
            other_row(env, n, env.order[env.lay * rows + n]).start()
        return [], []

    def emit_first(env, r, total):
        env.keep[r], env.send[r] = halves(env, total)
        env.mine[r] = total.astype(BF16)

    first, first_other, pieces = [None] * 2, [None] * 2, [None] * 2
    for q in range(2):
        outputs = {"keep": held(narrow, F32), "send": held(narrow, F32), "mine": held(wide, BF16)}
        out = product(
            f"product_0_{q}",
            False,
            tables,
            blocks,
            ([halo[q]], [mine[q]], [partner[q]]),
            {"other": in_hbm(other)} if q == 0 else {},
            {"blocks": held(blocks.shape, BF16), **outputs} if q == 0 else outputs,
            {"row_sems": pltpu.SemaphoreType.DMA((rows,))} if q == 0 else {},
            emit_first,
            before=start_rows if q == 0 else None,
            arrive=other_row if q == 0 else None,
            aliases=[("blocks_in", "blocks")] if q == 0 else (),
        )
        blocks = out.get("blocks", blocks)
        first[q] = out["keep"]
        first_other[q] = swap(out["send"])
        swapped = swap(out["mine"])
        pieces[q] = ([cross(out["mine"])], [out["mine"]], [swapped])

    def fill_rest(env):
        copies = []
        for n, source in enumerate((env.values, env.other)):
            at = (env.lay if n == 0 else 1 - env.lay) * slots
            copies.append(
                pltpu.make_async_copy(
                    source.at[pl.ds((1 - env.lay) * rows, rows)], env.rest.at[:, pl.ds(at, slots)], env.sems.at[2 + n]
                )
            )
        return copies

    def emit_second(env, r, total):
        keep, send = halves(env, total)
        env.keep[r], env.send[r] = keep.astype(BF16), send.astype(BF16)

    second, far, near, second_other = [None] * 2, [None] * 2, [None] * 2, [None] * 2
    for q in range(2):
        out = product(
            f"product_1_{q}",
            False,
            tables,
            blocks,
            pieces[q],
            {},
            {"keep": held(narrow, BF16), "send": held(narrow, BF16)},
            {},
            emit_second,
            after=[first[1], first_other[0]] if q == 0 else [first_other[1]],
        )
        second[q] = out["keep"]
        second_other[q] = swap(out["send"])
        near[q] = cross(out["send"])
        far[q] = pass_on(out["keep"])

    near[0], far[0], second_other[0] = together(near[0], far[0], second_other[0])

    target_shape = (jax.ShapeDtypeStruct((2 * rows, size, columns), F32), ANY)

    def load_first(env):
        return [
            pltpu.make_async_copy(part, env.first_buf.at[:, :, pl.ds(q * half, half)], env.sems.at[q])
            for q, part in enumerate((env.first_0, env.first_1))
        ], []

    def emit_last(env, r, total):
        env.kept[r] = 1.5 * env.first_buf[r] - 0.5 * total

    def finish_half(other_half):
        def finish_last(env, r):
            side = 1 - env.lay if other_half else env.lay
            return pltpu.make_async_copy(env.kept.at[r], env.target.at[side * rows + r], env.out_sems.at[r])

        return finish_last

    buffers = {
        "kept": pltpu.VMEM(wide, F32),
        "first_buf": pltpu.VMEM(wide, F32),
        "out_sems": pltpu.SemaphoreType.DMA((rows,)),
    }
    out = product(
        "product_2_own",
        False,
        tables,
        blocks,
        (near, second, second_other),
        {**dict(zip(("first_0", "first_1"), first)), "values": in_hbm(values), "other": in_hbm(other)},
        {"target": target_shape, "rest": held(blocks.shape, BF16)},
        buffers,
        emit_last,
        before=lambda env: (load_first(env)[0], fill_rest(env)),
        finish=finish_half(False),
    )
    target = product(
        "product_2_other",
        True,
        tables,
        out["rest"],
        (far, second_other, second),
        {**dict(zip(("first_0", "first_1"), first_other)), "target_in": out["target"]},
        {"target": target_shape},
        buffers,
        emit_last,
        before=load_first,
        finish=finish_half(True),
        aliases=[("target_in", "target")],
    )["target"]
    return target.reshape(2 * rows * size, columns)


def solution(mesh):
    chips = mesh.shape["row"] * mesh.shape["col"]
    return jax.shard_map(
        functools.partial(body, chips),
        mesh=mesh,
        in_specs=(
            P(("row", "col"), "layer", None, None),
            P(("row", "col"), "layer"),
            P(("row", "col")),
            P(("row", "col"), None),
        ),
        out_specs=P(("row", "col"), "layer"),
        check_vma=False,
    )
```

```python
import functools
import types

import jax
import jax.numpy as jnp
from jax import lax
from jax.experimental import pallas as pl
from jax.experimental.pallas import tpu as pltpu
from jax.sharding import PartitionSpec as P

AXES = ("layer", "row", "col")
GROUP = 4
TOGETHER = 4
F32, BF16 = jnp.float32, jnp.bfloat16
ANY = pl.BlockSpec(memory_space=pl.ANY)
SCALARS = pl.BlockSpec(memory_space=pltpu.SMEM)
RESIDENT = pl.BlockSpec(memory_space=pltpu.VMEM)


def in_vmem(x):
    return pltpu.with_memory_space_constraint(x, pltpu.VMEM)


def in_hbm(x):
    return pltpu.with_memory_space_constraint(x, pltpu.HBM)


def start_all(copies):
    for copy in copies:
        copy.start()


def wait_all(copies):
    for copy in copies:
        copy.wait()


def run_copies(copies):
    start_all(copies)
    wait_all(copies)


def small_cost():
    return pl.CostEstimate(flops=0, bytes_accessed=1024, transcendentals=0)


def stage_columns(vec, meta, own, after=()):
    rows, size, columns = vec.shape[0] // 2, vec.shape[1], vec.shape[2] // 2
    half = columns // 2
    share = 4

    def kernel(meta, vec, *refs):
        left, right, whole, load_sems, store_sems = refs[-5:]
        at = (meta[0] if own else 1 - meta[0]) * rows
        loads, stores = [], []
        for n in range(rows // share):
            part = pl.ds(n * share, share)
            loads.append(pltpu.make_async_copy(vec.at[pl.ds(at + n * share, share)], whole.at[part], load_sems.at[n]))
            stores.append(
                [
                    pltpu.make_async_copy(
                        whole.at[part, :, pl.ds((2 * h + piece) * half, half)],
                        out.at[part, :, pl.ds(h * half, half)],
                        store_sems.at[n, piece, h],
                    )
                    for piece, out in enumerate((left, right))
                    for h in range(2)
                ]
            )
        start_all(loads)
        for load, some in zip(loads, stores):
            load.wait()
            start_all(some)
        for some in stores:
            wait_all(some)

    shape = (rows, size, columns)
    return pl.pallas_call(
        kernel,
        out_shape=[jax.ShapeDtypeStruct(shape, BF16) if own else pltpu.VMEM(shape, BF16)] * 2,
        in_specs=[SCALARS, ANY] + [ANY] * len(after),
        out_specs=[ANY if own else RESIDENT] * 2,
        scratch_shapes=[
            pltpu.VMEM((rows, size, 2 * columns), BF16),
            pltpu.SemaphoreType.DMA((rows // share,)),
            pltpu.SemaphoreType.DMA((rows // share, 2, 2)),
        ],
        compiler_params=pltpu.CompilerParams(vmem_limit_bytes=3 * 2**20),
        cost_estimate=small_cost(),
        name="stage_columns",
    )(meta, in_hbm(vec), *after)


def fill_own(values, counts, meta, after):
    rows, slots, size = values.shape[0] // 2, values.shape[1], values.shape[2]

    def kernel(meta, counts, values, after, blocks, order, sem):
        lay = meta[0]
        copy = pltpu.make_async_copy(
            values.at[pl.ds(lay * rows, rows)], blocks.at[:, pl.ds(lay * slots, slots)], sem.at[0]
        )
        copy.start()
        for base in (0, rows):
            count = [counts[base + r] for r in range(rows)]
            rank = [jnp.int32(0)] * rows
            for i in range(rows):
                for j in range(i + 1, rows):
                    later = (count[j] > count[i]).astype(jnp.int32)
                    rank[i] += later
                    rank[j] += 1 - later
            for r in range(rows):
                order[base + rank[r]] = r
        copy.wait()

    return pl.pallas_call(
        kernel,
        out_shape=[
            pltpu.VMEM((rows, 2 * slots, size, size), BF16),
            jax.ShapeDtypeStruct((2 * rows,), jnp.int32),
        ],
        in_specs=[SCALARS, SCALARS, ANY, ANY],
        out_specs=[RESIDENT, SCALARS],
        scratch_shapes=[pltpu.SemaphoreType.DMA((1,))],
        compiler_params=pltpu.CompilerParams(vmem_limit_bytes=4 * 2**20),
        cost_estimate=small_cost(),
        name="fill_own",
    )(meta, counts, in_hbm(values), after)


def make_table(cols, cols_other, meta):
    slots, rows = cols.shape[0], cols.shape[1] // 2

    def kernel(meta, cols, cols_other, tab):
        for low in range(2):
            place = jnp.where(meta[0] == low, cols[...], cols_other[...]) - meta[1]
            upper = lax.broadcasted_iota(jnp.int32, place.shape, 1) >= rows
            turned = jnp.where(place < rows, place + 2 * rows, jnp.where(place < 2 * rows, place, place - 2 * rows))
            tab[low * slots : (low + 1) * slots, :] = jnp.where(upper, turned, place + rows)

    return pl.pallas_call(
        kernel,
        out_shape=jax.ShapeDtypeStruct((2 * slots, 2 * rows), jnp.int32),
        in_specs=[SCALARS, RESIDENT, RESIDENT],
        out_specs=RESIDENT,
        compiler_params=pltpu.CompilerParams(vmem_limit_bytes=2**20),
        cost_estimate=small_cost(),
        name="make_table",
    )(meta, cols, cols_other)


def together(*arrays):
    def kernel(*refs):
        del refs

    return pl.pallas_call(
        kernel,
        out_shape=[jax.ShapeDtypeStruct(x.shape, x.dtype) for x in arrays],
        in_specs=[ANY] * len(arrays),
        out_specs=[ANY] * len(arrays),
        input_output_aliases={n: n for n in range(len(arrays))},
        compiler_params=pltpu.CompilerParams(vmem_limit_bytes=2**20),
        cost_estimate=small_cost(),
        name="together",
    )(*arrays)


def product(label, other_half, tables, blocks, pieces, extras, outputs, scratch, emit, before=None, arrive=None, finish=None, aliases=(), after=()):
    rows, size, width = pieces[0][0].shape
    parts = len(pieces[0])
    columns = parts * width
    total_slots = blocks.shape[1]
    flat = [part for piece in pieces for part in piece]
    names = ["tab", "cnt", "order", "meta", "blocks_in"] + [f"piece{n}" for n in range(len(flat))]
    extras = {**extras, **{f"after{n}": x for n, x in enumerate(after)}}
    names += list(extras) + list(outputs) + ["field", "in_sems", "sems"] + list(scratch)

    def kernel(*refs):
        env = types.SimpleNamespace(**dict(zip(names, refs)))
        env.lay = env.meta[0]
        env.rows, env.half = rows, columns // 2
        env.blocks = getattr(env, "blocks", env.blocks_in)
        copies = [
            pltpu.make_async_copy(
                getattr(env, f"piece{n}"),
                env.field.at[pl.ds(n // parts * rows, rows), :, pl.ds(n % parts * width, width)],
                env.in_sems.at[n],
            )
            for n in range(len(flat))
        ]
        base = (1 - env.lay if other_half else env.lay) * rows
        now, later = before(env) if before else ([], [])
        start_all(copies + now + later)
        wait_all(copies + now)

        def some_rows(i, carry):
            picked = [env.order[base + i * TOGETHER + j] for j in range(TOGETHER)]
            counts = [env.cnt[base + r] for r in picked]
            if arrive:
                for j, r in enumerate(picked):
                    arrive(env, i * TOGETHER + j, r).wait()
            used = (counts[0] + (GROUP - 1)) // GROUP
            for m in range(1, total_slots // GROUP + 1):

                @pl.when(used == m)
                def _():
                    for r, count in zip(picked, counts):
                        left, right = [], []
                        for k in range(m * GROUP):
                            block = env.blocks[r, k]
                            left.append(jnp.where(k < count, block, jnp.zeros_like(block)))
                            right.append(env.field[env.tab[k, base + r]])
                        emit(
                            env,
                            r,
                            jnp.dot(
                                jnp.concatenate(left, axis=1),
                                jnp.concatenate(right, axis=0),
                                preferred_element_type=F32,
                            ),
                        )

            if finish:
                for r in picked:
                    finish(env, r).start()
            return carry

        lax.fori_loop(0, rows // TOGETHER, some_rows, 0)
        if finish:

            def await_row(r, carry):
                finish(env, r).wait()
                return carry

            lax.fori_loop(0, rows, await_row, 0)
        wait_all(later)

    inputs = [in_vmem(blocks)] + flat + list(extras.values())
    result = pl.pallas_call(
        kernel,
        out_shape=[shape for shape, _ in outputs.values()],
        in_specs=[SCALARS] * 4
        + [RESIDENT]
        + [ANY] * len(flat)
        + [RESIDENT if name.startswith("first_") else ANY for name in extras],
        out_specs=[spec for _, spec in outputs.values()],
        scratch_shapes=[
            pltpu.VMEM((len(pieces) * rows, size, columns), BF16),
            pltpu.SemaphoreType.DMA((len(flat),)),
            pltpu.SemaphoreType.DMA((4,)),
        ]
        + list(scratch.values()),
        input_output_aliases={names.index(i): list(outputs).index(o) for i, o in aliases},
        compiler_params=pltpu.CompilerParams(vmem_limit_bytes=10 * 2**20),
        cost_estimate=small_cost(),
        name=label,
    )(*tables, *inputs)
    return dict(zip(outputs, result))


def body(chips, values, cols, counts, vectors):
    rows = values.shape[0] // 2
    slots, size = values.shape[1], values.shape[2]
    columns = vectors.shape[1] // 2
    half = columns // 2
    lay = lax.axis_index("layer").astype(jnp.int32)
    start = lax.axis_index(("row", "col")).astype(jnp.int32) * 2 * rows
    up = [(chips + i, i + 1) for i in range(chips - 1)]
    across = up + [(b, a) for a, b in up]
    within = [(i, chips + i) for i in range(chips)] + [(chips + i, i) for i in range(chips)]
    along = [(i + 1, i) for i in range(chips - 1)] + [(chips + i, chips + i + 1) for i in range(chips - 1)]
    cross = lambda x: lax.ppermute(x, AXES, across)
    swap = lambda x: lax.ppermute(x, AXES, within)
    pass_on = lambda x: lax.ppermute(x, AXES, along)

    meta = jnp.stack([lay, start])
    vec = vectors.reshape(2 * rows, size, 2 * columns)
    other = swap(values)
    mine = list(stage_columns(vec, meta, True))
    halo = [cross(mine[q]) for q in range(2)]
    cols = cols.T
    cols_other = swap(cols)
    partner = list(stage_columns(vec, meta, False, [mine[0]]))
    blocks, order = fill_own(values, counts, meta, mine[0])
    tables = (make_table(cols, cols_other, meta), counts, order, meta)

    wide, narrow = (rows, size, columns), (rows, size, half)
    held = lambda shape, dtype: (pltpu.VMEM(shape, dtype), RESIDENT)

    def halves(env, x):
        left, right = x[:, : env.half], x[:, env.half :]
        return jnp.where(env.lay == 0, left, right), jnp.where(env.lay == 0, right, left)

    def other_row(env, n, r):
        return pltpu.make_async_copy(
            env.other.at[env.lay * rows + r], env.blocks.at[r, pl.ds((1 - env.lay) * slots, slots)], env.row_sems.at[n]
        )

    def start_rows(env):
        for n in range(rows):
            other_row(env, n, env.order[env.lay * rows + n]).start()
        return [], []

    def emit_first(env, r, total):
        env.keep[r], env.send[r] = halves(env, total)
        env.mine[r] = total.astype(BF16)

    first, first_other, pieces = [None] * 2, [None] * 2, [None] * 2
    for q in range(2):
        outputs = {"keep": held(narrow, F32), "send": held(narrow, F32), "mine": held(wide, BF16)}
        out = product(
            f"product_0_{q}",
            False,
            tables,
            blocks,
            ([halo[q]], [mine[q]], [partner[q]]),
            {"other": in_hbm(other)} if q == 0 else {},
            {"blocks": held(blocks.shape, BF16), **outputs} if q == 0 else outputs,
            {"row_sems": pltpu.SemaphoreType.DMA((rows,))} if q == 0 else {},
            emit_first,
            before=start_rows if q == 0 else None,
            arrive=other_row if q == 0 else None,
            aliases=[("blocks_in", "blocks")] if q == 0 else (),
        )
        blocks = out.get("blocks", blocks)
        first[q] = out["keep"]
        first_other[q] = swap(out["send"])
        swapped = swap(out["mine"])
        pieces[q] = ([cross(out["mine"])], [out["mine"]], [swapped])

    def fill_rest(env):
        copies = []
        for n, source in enumerate((env.values, env.other)):
            at = (env.lay if n == 0 else 1 - env.lay) * slots
            copies.append(
                pltpu.make_async_copy(
                    source.at[pl.ds((1 - env.lay) * rows, rows)], env.rest.at[:, pl.ds(at, slots)], env.sems.at[2 + n]
                )
            )
        return copies

    def emit_second(env, r, total):
        keep, send = halves(env, total)
        env.keep[r], env.send[r] = keep.astype(BF16), send.astype(BF16)

    second, far, near, second_other = [None] * 2, [None] * 2, [None] * 2, [None] * 2
    for q in range(2):
        out = product(
            f"product_1_{q}",
            False,
            tables,
            blocks,
            pieces[q],
            {},
            {"keep": held(narrow, BF16), "send": held(narrow, BF16)},
            {},
            emit_second,
            after=[first[1], first_other[0]] if q == 0 else [first_other[1]],
        )
        second[q] = out["keep"]
        second_other[q] = swap(out["send"])
        near[q] = cross(out["send"])
        far[q] = pass_on(out["keep"])

    near[0], far[0], second_other[0] = together(near[0], far[0], second_other[0])

    target_shape = (jax.ShapeDtypeStruct((2 * rows, size, columns), F32), ANY)

    def emit_last(env, r, total):
        env.kept[r] = 1.5 * jnp.concatenate([env.first_0[r], env.first_1[r]], axis=1) - 0.5 * total

    def finish_half(other_half):
        def finish_last(env, r):
            side = 1 - env.lay if other_half else env.lay
            return pltpu.make_async_copy(env.kept.at[r], env.target.at[side * rows + r], env.out_sems.at[r])

        return finish_last

    buffers = {
        "kept": pltpu.VMEM(wide, F32),
        "out_sems": pltpu.SemaphoreType.DMA((rows,)),
    }
    out = product(
        "product_2_own",
        False,
        tables,
        blocks,
        (near, second, second_other),
        {**dict(zip(("first_0", "first_1"), map(in_vmem, first))), "values": in_hbm(values), "other": in_hbm(other)},
        {"target": target_shape, "rest": held(blocks.shape, BF16)},
        buffers,
        emit_last,
        before=lambda env: ([], fill_rest(env)),
        finish=finish_half(False),
    )
    target = product(
        "product_2_other",
        True,
        tables,
        out["rest"],
        (far, second_other, second),
        {**dict(zip(("first_0", "first_1"), map(in_vmem, first_other))), "target_in": out["target"]},
        {"target": target_shape},
        buffers,
        emit_last,
        finish=finish_half(True),
        aliases=[("target_in", "target")],
    )["target"]
    return target.reshape(2 * rows * size, columns)


def solution(mesh):
    chips = mesh.shape["row"] * mesh.shape["col"]
    return jax.shard_map(
        functools.partial(body, chips),
        mesh=mesh,
        in_specs=(
            P(("row", "col"), "layer", None, None),
            P(("row", "col"), "layer"),
            P(("row", "col")),
            P(("row", "col"), None),
        ),
        out_specs=P(("row", "col"), "layer"),
        check_vma=False,
    )
```
